32 devices in a mesh: ctx: 16 (over z, y, x), head: 2 (over core).
Axes of the slice: x: 2, y: 2, z: 4, core: 2. Of those that a mesh axis runs over, the one named last changes fastest.
Arguments:
- queries: bfloat16 [16384, 4096], P(('ctx', 'head')), may hold values from -400 to 400
- key_states: bfloat16 [16384, 1024], P(('ctx', 'head')), may hold values from -5 to 5
- value_states: bfloat16 [16384, 1024], P(('ctx', 'head')), may hold values from -6 to 6
- selection: int32 [32, 8, 4], replicated, may hold values from -1 to 31, as said below
Outputs:
- attended: bfloat16 [16384, 4096], P(('ctx', 'head'))
The draws below stay inside these ranges and needn't reach their ends.
Inputs may be any that keep to these rules, and one draw needn't show every extreme that they name: `selection`: column 0 of row b is b. Columns 1 to 3 name distinct blocks below b, or -1 where none is named. Take the rows of the 2 blocks of one ctx index c (rows c * 2 to c * 2 + 1) and the 4 key-value heads of one head index (heads h * 4 to h * 4 + 3): the named blocks among them that belong to other ctx indices (block // 2 != c) lie on distinct ctx indices, so at most one block is named from any other ctx index; in every draw some ctx index names one block from each of several others.
All inputs are finite; a program needn't handle non-finite values.
Results may differ from the reference program's by a relative error of at most 0.004.
Values may be sent and summed in bfloat16 or wider, within the bound.
No kernel may reach another device: no remote copies, remote signals or barrier semaphores. Data moves between devices by JAX's collectives and lax.ppermute only.
A program may use at most 128 MiB of HBM per device.

```python
import math
import jax
import jax.numpy as jnp
from jax import lax

QH = 32
KVH = 8
HD = 128
BLK = 512
TOPK = 3
BPD = 2
KVG = 4
TOKENS = 16384
NBLK = 32


def attention_fields(key):
    key_field = jnp.clip(jax.random.normal(jax.random.fold_in(key, 21), (TOKENS, KVH * HD)), -5.0, 5.0)
    query_field = jnp.clip(jax.random.normal(jax.random.fold_in(key, 22), (TOKENS, QH * HD)), -6.0, 6.0)
    return (query_field, key_field)


def draw_queries(key, part):
    return attention_fields(key)[0].astype(jnp.bfloat16)


def draw_key_states(key, part):
    return attention_fields(key)[1].astype(jnp.bfloat16)


def draw_selection(key, part):
    ctx_count = NBLK // BPD
    group_count = KVH // KVG
    slot_count = BPD * KVG * TOPK
    devices = jnp.arange(ctx_count, dtype=jnp.int32)
    peer_score = jax.random.randint(jax.random.fold_in(key, 11), (ctx_count, group_count, ctx_count), 0, 1 << 20)
    peer_score = jnp.where(devices[None, None, :] < devices[:, None, None], peer_score, 1 << 21)
    peer_order = jnp.argsort(peer_score * ctx_count + devices[None, None, :], axis=-1).astype(jnp.int32)
    slot_ids = jnp.arange(slot_count, dtype=jnp.int32)
    slot_score = jax.random.randint(jax.random.fold_in(key, 12), (ctx_count, group_count, slot_count), 0, 1 << 20)
    slot_order = jnp.argsort(slot_score * slot_count + slot_ids[None, None, :], axis=-1).astype(jnp.int32)
    slot_rank = jnp.argsort(slot_order, axis=-1).astype(jnp.int32)
    remote = slot_rank < devices[:, None, None]
    peers = jnp.take_along_axis(peer_order, jnp.minimum(slot_rank, ctx_count - 1), axis=-1)
    inner = jax.random.randint(jax.random.fold_in(key, 14), (ctx_count, group_count, slot_count), 0, BPD)
    remote_block = (peers * BPD + inner).reshape(ctx_count, group_count, BPD, KVG, TOPK)
    remote_grid = remote.reshape(ctx_count, group_count, BPD, KVG, TOPK)
    local_flag = 1 - remote_grid.astype(jnp.int32)
    local_rank = jnp.cumsum(local_flag, axis=-1) - local_flag
    query_ids = jnp.arange(BPD, dtype=jnp.int32)[None, None, :, None, None]
    local_place = query_ids - 1 - local_rank
    local_block = jnp.where(local_place >= 0, devices[:, None, None, None, None] * BPD + local_place, -1)
    picks = jnp.where(remote_grid, remote_block, local_block)
    own_block = jnp.broadcast_to(devices[:, None, None, None, None] * BPD + query_ids, (ctx_count, group_count, BPD, KVG, 1))
    grid = jnp.concatenate([own_block, picks], axis=-1).astype(jnp.int32)
    return grid.transpose(0, 2, 1, 3, 4).reshape(NBLK, KVH, TOPK + 1)


def shard_levels(key, extent, shards, smallest, high):
    loudness, own = 1.0, jax.random.fold_in(key, 6)
    for dim, blocks in shards:
        heights = jnp.exp(jax.random.uniform(jax.random.fold_in(own, dim), (blocks,), jnp.float32, smallest / len(shards), high / len(shards)))
        loudness = loudness * jnp.repeat(heights, extent[dim] // blocks).reshape([-1 if axis == dim else 1 for axis in range(len(extent))])
    return loudness


def noise(rng, shape, spread, reach, pieces=(), kind=jnp.bfloat16):
    drawn = spread * jax.random.normal(rng, shape, jnp.float32)
    if pieces:
        drawn = drawn * shard_levels(rng, shape, pieces, -0.22, 0.18)
    return jnp.clip(drawn, -reach, reach).astype(kind)


def setup_inputs(seed: int = 0) -> dict:
    key_list = jax.random.split(jax.random.key(seed), 5)
    queries = draw_queries(jax.random.fold_in(key_list[4], 71), 0)
    key_states = draw_key_states(jax.random.fold_in(key_list[4], 71), 0)
    value_states = noise(key_list[2], (TOKENS, KVH * HD), 1.0, 6.0, ((0, 32),))
    selection = draw_selection(jax.random.fold_in(key_list[4], 71), 0)
    return {"queries": queries, "key_states": key_states, "value_states": value_states, "selection": selection}


def reference(queries, key_states, value_states, selection):
    group_size = QH // KVH
    scaling = 1.0 / math.sqrt(HD)
    query_blocks = queries.reshape(NBLK, BLK, KVH, group_size, HD)
    key_blocks = key_states.reshape(NBLK, BLK, KVH, HD).transpose(2, 0, 1, 3)
    value_blocks = value_states.reshape(NBLK, BLK, KVH, HD).transpose(2, 0, 1, 3)
    causal = jnp.arange(BLK)[:, None] >= jnp.arange(BLK)[None, :]
    head_rows = jnp.arange(KVH)[:, None]

    def one_block(block_index):
        query_now = query_blocks[block_index].astype(jnp.float32)
        own_keys = key_blocks[:, block_index].astype(jnp.float32)
        own_values = value_blocks[:, block_index].astype(jnp.float32)
        picks = selection[block_index, :, 1:]
        present = picks >= 0
        safe_picks = jnp.where(present, picks, 0).astype(jnp.int32)
        far_keys = key_blocks[head_rows, safe_picks].astype(jnp.float32)
        far_values = value_blocks[head_rows, safe_picks].astype(jnp.float32)
        own_scores = jnp.einsum('tkgd,kud->kgtu', query_now, own_keys) * scaling
        own_scores = jnp.where(causal[None, None], own_scores, -jnp.inf)
        far_scores = jnp.einsum('tkgd,kjud->kgtju', query_now, far_keys) * scaling
        far_scores = jnp.where(present[:, None, None, :, None], far_scores, -jnp.inf)
        peak = jnp.maximum(lax.optimization_barrier(jnp.max(own_scores, axis=-1)), lax.optimization_barrier(jnp.max(far_scores, axis=(-2, -1))))
        own_weights = jnp.exp(own_scores - peak[..., None])
        far_weights = jnp.exp(far_scores - peak[..., None, None])
        denominator = lax.optimization_barrier(jnp.sum(own_weights, axis=-1)) + lax.optimization_barrier(jnp.sum(far_weights, axis=(-2, -1)))
        own_rounded = lax.optimization_barrier(own_weights.astype(jnp.bfloat16)).astype(jnp.float32)
        far_rounded = lax.optimization_barrier(far_weights.astype(jnp.bfloat16)).astype(jnp.float32)
        numerator = jnp.einsum('kgtu,kud->kgtd', own_rounded, own_values)
        numerator = numerator + jnp.einsum('kgtju,kjud->kgtd', far_rounded, far_values)
        result = (numerator / denominator[..., None]).astype(jnp.bfloat16)
        return result.transpose(2, 0, 1, 3)
    stacked = lax.map(one_block, jnp.arange(NBLK, dtype=jnp.int32))
    return stacked.reshape(TOKENS, QH * HD)
```

```python
import functools
import math

import jax
import jax.numpy as jnp
import numpy as np
from jax import lax
from jax.experimental import pallas as pl
from jax.experimental.pallas import tpu as pltpu
from jax.sharding import PartitionSpec as P

QH = 32
KVH = 8
HD = 128
BLK = 512
TOPK = 3
GROUP = QH // KVH
KVG = KVH // 2
WIDE = GROUP * HD
ROWS = GROUP * BLK
SCALE = math.log2(math.e) / math.sqrt(HD)
TILE = 256
VMEM = pltpu.VMEM
ANY = pl.ANY


def patterns(peers):
    fast = 4 if peers % 4 == 0 else 1
    slow = peers // fast
    far = sorted(range(1, slow), key=lambda d: -min(d, slow - d))
    order = [(0, m) for m in range(1, fast)]
    order += [(d, m) for m in range(fast) for d in far]
    count = 5
    edges = [round(i * len(order) / count) for i in range(count + 1)]
    return fast, slow, order, list(zip(edges[:-1], edges[1:]))


def pairs_of(fast, slow, step, flip):
    pairs = []
    for s in range(slow - step):
        for f in range(fast):
            source, target = s * fast + f, (s + step) * fast + (f ^ flip)
            if target > source:
                pairs.append((source, target))
    return pairs


def fold(q, k, vx, m_old, l_old, acc_old, mask=None):
    scores = lax.dot_general(q, k, (((1,), (1,)), ((), ())), preferred_element_type=jnp.float32)
    if mask is not None:
        scores = jnp.where(mask, scores, -1e30)
    m_new = jnp.max(scores, axis=1, keepdims=True)
    if m_old is not None:
        m_new = jnp.maximum(m_old, m_new)
    weights = jnp.exp2((scores - m_new) * SCALE).astype(jnp.bfloat16)
    both = jnp.dot(weights, vx, preferred_element_type=jnp.float32)
    acc, l_new = both[:, :HD], both[:, HD:]
    if m_old is not None:
        alpha = jnp.exp2((m_old - m_new) * SCALE)
        acc = acc + acc_old * alpha
        l_new = l_new + l_old * alpha
    return m_new, l_new, acc


def packed(m, l):
    lane = lax.broadcasted_iota(jnp.int32, l.shape, 1)
    return jnp.where(lane < HD // 2, m, l)


def cut_kernel(fast, slow, order, meta, key, value, okey, ovalue, *rest):
    outs, sems = rest[:-1], rest[-1]
    me, side = meta[0], meta[1]
    s_me, f_me = me // fast, me % fast

    def each(act):
        for j, (step, flip) in enumerate(order):
            f_to = f_me ^ flip
            target = (s_me + step) * fast + f_to
            fine = jnp.logical_and(s_me + step < slow, target > me)
            code = jnp.where(fine, meta[2 + jnp.where(fine, target, 0)], 0) - 1
            block, head = code // KVH, code % KVH
            col = pl.multiple_of(jnp.maximum(head, 0) * HD, HD)
            for t, (here, there) in enumerate(((key, okey), (value, ovalue))):
                to = outs[j].at[pl.ds(t * BLK, BLK), :]
                mine = pltpu.make_async_copy(here.at[:, pl.ds(col, HD)], to, sems.at[j, t])
                other = pltpu.make_async_copy(there.at[:, pl.ds(col, HD)], to, sems.at[j, t])
                act(jnp.logical_and(code >= 0, block == side), mine)
                act(jnp.logical_and(code >= 0, block != side), other)

    def start(flag, copy):
        pl.when(flag)(copy.start)

    def wait(flag, copy):
        pl.when(flag)(copy.wait)

    each(start)
    each(wait)


def own_kernel(local_at, meta, q, k, v, ok, ov, acc_out, ml_out, out, vx):
    g = pl.program_id(0)
    vx[:, HD:] = jnp.ones((BLK, HD), jnp.bfloat16)
    vx[:, :HD] = v[...]
    for r in range(BLK // TILE):
        keys = (r + 1) * TILE
        row = lax.broadcasted_iota(jnp.int32, (TILE, keys), 0) + r * TILE
        mask = row >= lax.broadcasted_iota(jnp.int32, (TILE, keys), 1)
        for j in range(GROUP):
            tile = q[r * TILE : (r + 1) * TILE, j * HD : (j + 1) * HD]
            m, l, acc = fold(tile, k[:keys, :], vx[:keys, :], None, None, None, mask)
            at = pl.ds(j * BLK + r * TILE, TILE)
            acc_out[0, at, :] = acc
            ml_out[0, at, :] = packed(m, l)

    @pl.when(meta[local_at + g] > 0)
    def _():
        vx[:, :HD] = ov[...]
        for r in range(BLK // TILE):
            for j in range(GROUP):
                tile = q[r * TILE : (r + 1) * TILE, j * HD : (j + 1) * HD]
                at = pl.ds(j * BLK + r * TILE, TILE)
                ml = ml_out[0, at, :]
                m, l, acc = fold(
                    tile, ok[...], vx[...], ml[:, :1], ml[:, HD // 2 : HD // 2 + 1], acc_out[0, at, :]
                )
                acc_out[0, at, :] = acc
                ml_out[0, at, :] = packed(m, l)

    for j in range(GROUP):
        at = pl.ds(j * BLK, BLK)
        total = ml_out[0, at, :][:, HD // 2 : HD // 2 + 1]
        out[:, j * HD : (j + 1) * HD] = (acc_out[0, at, :] / total).astype(jnp.bfloat16)


def far_kernel(count, work_at, here_at, later_at, meta, *refs):
    arrived, swapped = refs[:count], refs[count]
    q_hbm, acc_hbm, ml_hbm, out_hbm = refs[count + 1 : count + 5]
    acc_new, ml_new, out_new = refs[count + 5 : count + 8]
    qs, accs, mls, outs, vx, seen, in_sem, out_sem = refs[count + 8 :]

    def loads(g):
        return (
            pltpu.make_async_copy(q_hbm.at[:, pl.ds(pl.multiple_of(g * WIDE, WIDE), WIDE)], qs.at[g], in_sem.at[g, 0]),
            pltpu.make_async_copy(acc_hbm.at[g], accs.at[g], in_sem.at[g, 1]),
            pltpu.make_async_copy(ml_hbm.at[g], mls.at[g], in_sem.at[g, 2]),
        )

    def stores(g):
        return (
            pltpu.make_async_copy(accs.at[g], acc_new.at[g], out_sem.at[g, 0]),
            pltpu.make_async_copy(mls.at[g], ml_new.at[g], out_sem.at[g, 1]),
        )

    def finish(g):
        return pltpu.make_async_copy(
            outs.at[g], out_new.at[:, pl.ds(pl.multiple_of(g * WIDE, WIDE), WIDE)], out_sem.at[g, 2]
        )

    for g in range(KVH):
        seen[g] = 0

        @pl.when(meta[here_at + g] > 0)
        def _():
            for copy in loads(g):
                copy.start()

    vx[:, HD:] = jnp.ones((BLK, HD), jnp.bfloat16)

    def piece(g, source, base):
        @pl.when(seen[g] == 0)
        def _():
            for copy in loads(g):
                copy.wait()

        vx[:, :HD] = source[base + BLK : base + 2 * BLK, :]

        def rows(i, carry):
            at = pl.ds(pl.multiple_of(i * TILE, TILE), TILE)
            j, r = i // (BLK // TILE), i % (BLK // TILE)
            tile = qs[g, pl.ds(pl.multiple_of(r * TILE, TILE), TILE), pl.ds(pl.multiple_of(j * HD, HD), HD)]
            ml = mls[g, at, :]
            m, l, acc = fold(
                tile, source[base : base + BLK, :], vx[...], ml[:, :1], ml[:, HD // 2 : HD // 2 + 1], accs[g, at, :]
            )
            accs[g, at, :] = acc
            mls[g, at, :] = packed(m, l)
            return carry

        lax.fori_loop(0, ROWS // TILE, rows, 0, unroll=2)
        seen[g] = seen[g] + 1
        done = seen[g] == meta[here_at + g]
        last = meta[later_at + g] == 0

        @pl.when(jnp.logical_and(done, jnp.logical_not(last)))
        def _():
            for copy in stores(g):
                copy.start()

        @pl.when(jnp.logical_and(done, last))
        def _():
            for j in range(GROUP):
                at = pl.ds(j * BLK, BLK)
                total = mls[g, at, :][:, HD // 2 : HD // 2 + 1]
                outs[g, :, j * HD : (j + 1) * HD] = (accs[g, at, :] / total).astype(jnp.bfloat16)
            finish(g).start()

    for i in range(count):
        for t, (source, base) in enumerate(((arrived[i], 0), (swapped, i * 2 * BLK))):
            g = meta[work_at + 2 * i + t]
            pl.when(g >= 0)(functools.partial(piece, g, source, base))

    for g in range(KVH):
        here = meta[here_at + g] > 0
        last = meta[later_at + g] == 0

        @pl.when(jnp.logical_and(here, jnp.logical_not(last)))
        def _():
            for copy in stores(g):
                copy.wait()

        @pl.when(jnp.logical_and(here, last))
        def _():
            finish(g).wait()


def body(queries, key, value, selection):
    me, side = lax.axis_index("ctx"), lax.axis_index("head")
    peers = lax.axis_size("ctx")
    fast, slow, order, groups = patterns(peers)
    steps = np.array([s for s, _ in order], np.int32)
    flips = np.array([f for _, f in order], np.int32)
    swap = [(0, 1), (1, 0)]
    okey, ovalue = lax.ppermute(key, "head", swap), lax.ppermute(value, "head", swap)

    picks = selection[:, :, 1:]
    asked = lax.dynamic_slice_in_dim(picks, side * KVG, KVG, 1)
    codes = (asked - 2 * me) * KVH + (side * KVG + jnp.arange(KVG, dtype=jnp.int32))[None, :, None] + 1
    wanted = jnp.max(
        jnp.where((asked >> 1) == me, codes, 0).reshape(peers, 2 * KVG * TOPK), axis=1
    )
    mine = lax.dynamic_slice_in_dim(picks, 2 * me + side, 1, 0)[0]
    owners = jnp.where(mine >= 0, mine >> 1, -1)
    local = jnp.any(owners == me, axis=1).astype(jnp.int32)
    s_from = me // fast - steps
    source = jnp.where(s_from >= 0, s_from * fast + ((me % fast) ^ flips), me)
    source = jnp.where(source < me, source, -2)
    heads = jnp.arange(KVH, dtype=jnp.int32)
    half = (heads // KVG) ^ side
    hit = jnp.any(owners[None, :, :] == source[:, None, None], axis=2)
    work = jnp.max(
        jnp.where(hit[:, None, :] & (half[None, None, :] == np.arange(2, dtype=np.int32)[None, :, None]), heads, -1),
        axis=2,
    )
    hits = hit.astype(jnp.int32)
    here = jnp.stack([jnp.sum(hits[a:b], axis=0) for a, b in groups])
    later = jnp.stack([jnp.sum(hits[b:], axis=0) for a, b in groups])
    meta = jnp.concatenate(
        [jnp.stack([me, side]).astype(jnp.int32), wanted, local, work.reshape(-1), here.reshape(-1), later.reshape(-1)]
    ).astype(jnp.int32)
    local_at = 2 + peers
    work_at = local_at + KVH
    here_at = work_at + 2 * len(order)
    later_at = here_at + KVH * len(groups)

    piece_shape = jax.ShapeDtypeStruct((2 * BLK, HD), jnp.bfloat16)
    sent = pl.pallas_call(
        functools.partial(cut_kernel, fast, slow, order),
        grid_spec=pltpu.PrefetchScalarGridSpec(
            num_scalar_prefetch=1,
            grid=(),
            in_specs=[pl.BlockSpec(memory_space=ANY)] * 4,
            out_specs=[pl.BlockSpec(memory_space=ANY)] * len(order),
            scratch_shapes=[pltpu.SemaphoreType.DMA((len(order), 2))],
        ),
        out_shape=[piece_shape] * len(order),
        cost_estimate=pl.CostEstimate(flops=0, bytes_accessed=len(order) << 19, transcendentals=0),
        name="cut",
    )(meta, key, value, okey, ovalue)
    landed = [lax.ppermute(x, "ctx", pairs_of(fast, slow, *p)) for x, p in zip(sent, order)]

    state = (
        jax.ShapeDtypeStruct((KVH, ROWS, HD), jnp.float32),
        jax.ShapeDtypeStruct((KVH, ROWS, HD), jnp.float32),
        jax.ShapeDtypeStruct((BLK, QH * HD), jnp.bfloat16),
    )
    kv_spec = pl.BlockSpec((BLK, HD), lambda g, _: (0, g))
    q_spec = pl.BlockSpec((BLK, WIDE), lambda g, _: (0, g))
    s_spec = pl.BlockSpec((1, ROWS, HD), lambda g, _: (g, 0, 0))
    piece_flops = 4 * ROWS * BLK * HD
    acc, ml, out = pl.pallas_call(
        functools.partial(own_kernel, local_at),
        grid_spec=pltpu.PrefetchScalarGridSpec(
            num_scalar_prefetch=1,
            grid=(KVH,),
            in_specs=[q_spec] + [kv_spec] * 4,
            out_specs=[s_spec, s_spec, q_spec],
            scratch_shapes=[VMEM((BLK, 2 * HD), jnp.bfloat16)],
        ),
        out_shape=state,
        compiler_params=pltpu.CompilerParams(vmem_limit_bytes=48 << 20),
        cost_estimate=pl.CostEstimate(
            flops=12 * piece_flops, bytes_accessed=28 << 20, transcendentals=12 * ROWS * BLK
        ),
        name="own",
    )(meta, queries, key, value, okey, ovalue)

    for n, (a, b) in enumerate(groups):
        count = b - a
        swapped = lax.ppermute(jnp.concatenate(landed[a:b], axis=0), "head", swap)
        acc, ml, out = pl.pallas_call(
            functools.partial(
                far_kernel, count, work_at + 2 * a, here_at + KVH * n, later_at + KVH * n
            ),
            grid_spec=pltpu.PrefetchScalarGridSpec(
                num_scalar_prefetch=1,
                grid=(),
                in_specs=[pl.BlockSpec(memory_space=VMEM)] * (count + 1) + [pl.BlockSpec(memory_space=ANY)] * 4,
                out_specs=[pl.BlockSpec(memory_space=ANY)] * 3,
                scratch_shapes=[
                    VMEM((KVH, BLK, WIDE), jnp.bfloat16),
                    VMEM((KVH, ROWS, HD), jnp.float32),
                    VMEM((KVH, ROWS, HD), jnp.float32),
                    VMEM((KVH, BLK, WIDE), jnp.bfloat16),
                    VMEM((BLK, 2 * HD), jnp.bfloat16),
                    pltpu.SMEM((KVH,), jnp.int32),
                    pltpu.SemaphoreType.DMA((KVH, 3)),
                    pltpu.SemaphoreType.DMA((KVH, 3)),
                ],
            ),
            out_shape=state,
            input_output_aliases={count + 3: 0, count + 4: 1, count + 5: 2},
            compiler_params=pltpu.CompilerParams(vmem_limit_bytes=48 << 20),
            cost_estimate=pl.CostEstimate(
                flops=count * piece_flops, bytes_accessed=count << 22, transcendentals=count * ROWS * BLK
            ),
            name="far",
        )(meta, *landed[a:b], swapped, queries, acc, ml, out)
    return out


def solution(mesh):
    placed = (P(("ctx", "head"), None), P(("ctx", "head"), None), P(("ctx", "head"), None), P())
    return jax.shard_map(
        body, mesh=mesh, in_specs=placed, out_specs=P(("ctx", "head"), None), check_vma=False
    )
```

```python
import functools
import math

import jax
import jax.numpy as jnp
import numpy as np
from jax import lax
from jax.experimental import pallas as pl
from jax.experimental.pallas import tpu as pltpu
from jax.sharding import PartitionSpec as P

QH = 32
KVH = 8
HD = 128
BLK = 512
TOPK = 3
GROUP = QH // KVH
KVG = KVH // 2
WIDE = GROUP * HD
ROWS = GROUP * BLK
SCALE = math.log2(math.e) / math.sqrt(HD)
TILE = 128
VMEM = pltpu.VMEM
ANY = pl.ANY


def patterns(peers):
    fast = 4 if peers % 4 == 0 else 1
    slow = peers // fast
    if (fast, slow) == (4, 4):
        order = [(2, 0), (1, 0), (3, 0), (2, 1), (1, 1), (3, 1), (2, 2), (0, 1), (1, 2), (0, 2), (3, 2), (2, 3), (0, 3)]
        order += [(1, 3), (3, 3)]
        edges = [0, 3, 6, 10, 13, 15]
    else:
        far = sorted(range(1, slow), key=lambda d: -min(d, slow - d))
        order = [(d, m) for m in range(fast) for d in far] + [(0, m) for m in range(1, fast)]
        edges = [round(i * len(order) / 5) for i in range(6)]
    return fast, slow, order, list(zip(edges[:-1], edges[1:]))


def pairs_of(fast, slow, step, flip):
    pairs = []
    for s in range(slow - step):
        for f in range(fast):
            source, target = s * fast + f, (s + step) * fast + (f ^ flip)
            if target > source:
                pairs.append((source, target))
    return pairs


def scores_of(k, q):
    return lax.dot_general(k, q, (((1,), (1,)), ((), ())), preferred_element_type=jnp.float32)


def total_of(vt, weights):
    return jnp.dot(vt, weights.astype(jnp.bfloat16), preferred_element_type=jnp.float32)


def cut_kernel(fast, slow, order, meta, key, value, okey, ovalue, *rest):
    outs, sems = rest[:-1], rest[-1]
    me, side = meta[0], meta[1]
    s_me, f_me = me // fast, me % fast

    def each(act):
        for j, (step, flip) in enumerate(order):
            f_to = f_me ^ flip
            target = (s_me + step) * fast + f_to
            fine = jnp.logical_and(s_me + step < slow, target > me)
            code = jnp.where(fine, meta[2 + jnp.where(fine, target, 0)], 0) - 1
            block, head = code // KVH, code % KVH
            col = pl.multiple_of(jnp.maximum(head, 0) * HD, HD)
            for t, (here, there) in enumerate(((key, okey), (value, ovalue))):
                to = outs[j].at[pl.ds(t * BLK, BLK), :]
                mine = pltpu.make_async_copy(here.at[:, pl.ds(col, HD)], to, sems.at[j, t])
                other = pltpu.make_async_copy(there.at[:, pl.ds(col, HD)], to, sems.at[j, t])
                act(jnp.logical_and(code >= 0, block == side), mine)
                act(jnp.logical_and(code >= 0, block != side), other)

    def start(flag, copy):
        pl.when(flag)(copy.start)

    def wait(flag, copy):
        pl.when(flag)(copy.wait)

    each(start)
    each(wait)


def own_kernel(local_at, meta, q, k, v, ok, ov, acc_out, stat_out, out, vt):
    g = pl.program_id(0)
    vt[...] = v[...].T
    for r in range(BLK // TILE):
        keys, at = (r + 1) * TILE, slice(r * TILE, (r + 1) * TILE)
        row = lax.broadcasted_iota(jnp.int32, (keys, TILE), 1) + r * TILE
        mask = row >= lax.broadcasted_iota(jnp.int32, (keys, TILE), 0)
        for j in range(GROUP):
            scores = scores_of(k[:keys, :], q[at, j * HD : (j + 1) * HD])
            scores = jnp.where(mask, scores, -1e30)
            m = jnp.max(scores, axis=0, keepdims=True)
            weights = jnp.exp2((scores - m) * SCALE)
            stat_out[0, j : j + 1, at] = m
            stat_out[0, GROUP + j : GROUP + j + 1, at] = jnp.sum(weights, axis=0, keepdims=True)
            acc_out[0, j, :, at] = total_of(vt[:, :keys], weights)

    @pl.when(meta[local_at + g] > 0)
    def _():
        vt[...] = ov[...].T
        fold(ok, lambda at, col: q[at, col], vt, acc_out.at[0], stat_out.at[0])

    for j in range(GROUP):
        total = stat_out[0, GROUP + j : GROUP + j + 1, :]
        out[:, j * HD : (j + 1) * HD] = (acc_out[0, j] / total).T.astype(jnp.bfloat16)


def fold(k, q_of, vt, acc, stat):
    for j in range(GROUP):
        for r in range(BLK // TILE):
            at = slice(r * TILE, (r + 1) * TILE)
            scores = scores_of(k[...], q_of(at, slice(j * HD, (j + 1) * HD)))
            m_old = stat[j : j + 1, at]
            m = jnp.maximum(m_old, jnp.max(scores, axis=0, keepdims=True))
            weights = jnp.exp2((scores - m) * SCALE)
            alpha = jnp.exp2((m_old - m) * SCALE)
            total = GROUP + j
            stat[j : j + 1, at] = m
            stat[total : total + 1, at] = stat[total : total + 1, at] * alpha + jnp.sum(weights, axis=0, keepdims=True)
            acc[j, :, at] = acc[j, :, at] * alpha + total_of(vt[...], weights)


def far_kernel(n_here, n_swap, n_pass, here_at, here_later, swap_at, swap_later, meta, *refs):
    arrived, refs = refs[:n_here], refs[n_here:]
    swapped, refs = refs[:n_swap], refs[n_swap:]
    q_hbm, acc_hbm, stat_hbm = refs[:3]
    refs = refs[4 + n_pass :]
    acc_new, stat_new, out_new = refs[:3]
    qs, accs, stats, outs, kv, vt, seen, here, later, kv_sem, in_sem, out_sem = refs[3 + n_pass :]
    each = n_swap and swapped[0].shape[0] // (2 * BLK)
    pieces = n_here + n_swap * each

    def wide(g):
        return pl.ds(pl.multiple_of(g * WIDE, WIDE), WIDE)

    def loads(g):
        return (
            pltpu.make_async_copy(q_hbm.at[:, wide(g)], qs.at[g], in_sem.at[g, 0]),
            pltpu.make_async_copy(acc_hbm.at[g], accs.at[g], in_sem.at[g, 1]),
            pltpu.make_async_copy(stat_hbm.at[g], stats.at[g], in_sem.at[g, 2]),
        )

    def stores(g):
        return (
            pltpu.make_async_copy(accs.at[g], acc_new.at[g], out_sem.at[g, 0]),
            pltpu.make_async_copy(stats.at[g], stat_new.at[g], out_sem.at[g, 1]),
        )

    def finish(g):
        return pltpu.make_async_copy(outs.at[g], out_new.at[:, wide(g)], out_sem.at[g, 2])

    def head_of(i):
        return meta[jnp.where(i < n_here, here_at + i, swap_at + i - n_here)]

    for g in range(KVH):
        seen[g] = 0
        here[g] = 0
        later[g] = 0

    for i in range(pieces):
        g = meta[here_at + i] if i < n_here else meta[swap_at + i - n_here]
        block = arrived[i] if i < n_here else swapped[0].at[pl.ds((i - n_here) * 2 * BLK, 2 * BLK), :]

        @pl.when(g >= 0)
        def _():
            pltpu.make_async_copy(block, kv.at[i], kv_sem.at[i]).start()

            @pl.when(here[g] == 0)
            def _():
                for copy in loads(g):
                    copy.start()

            here[g] = here[g] + 1

    def count(i, carry):
        g = meta[i]

        @pl.when(g >= 0)
        def _():
            later[g] = later[g] + 1

        return carry

    lax.fori_loop(*here_later, count, 0)
    lax.fori_loop(*swap_later, count, 0)

    def piece(i, carry):
        g = head_of(i)

        @pl.when(g >= 0)
        def _():
            @pl.when(seen[g] == 0)
            def _():
                for copy in loads(g):
                    copy.wait()

            pltpu.make_async_copy(kv.at[i], kv.at[i], kv_sem.at[i]).wait()
            vt[...] = kv[i, BLK:, :].T
            fold(
                kv.at[i, pl.ds(0, BLK), :], lambda at, col: qs[g, at, col], vt, accs.at[g], stats.at[g]
            )
            seen[g] = seen[g] + 1
            done = seen[g] == here[g]

            @pl.when(jnp.logical_and(done, later[g] > 0))
            def _():
                for copy in stores(g):
                    copy.start()

            @pl.when(jnp.logical_and(done, later[g] == 0))
            def _():
                for j in range(GROUP):
                    outs[g, :, j * HD : (j + 1) * HD] = (
                        (accs[g, j] / stats[g, GROUP + j : GROUP + j + 1, :]).T.astype(jnp.bfloat16)
                    )
                finish(g).start()

        return carry

    lax.fori_loop(0, pieces, piece, 0)

    for g in range(KVH):
        used = here[g] > 0

        @pl.when(jnp.logical_and(used, later[g] > 0))
        def _():
            for copy in stores(g):
                copy.wait()

        @pl.when(jnp.logical_and(used, later[g] == 0))
        def _():
            finish(g).wait()


def pack_kernel(*refs):
    arrived, joined = refs[: (len(refs) - 3)], refs[-2]
    for i, x in enumerate(arrived):
        joined[i * 2 * BLK : (i + 1) * 2 * BLK, :] = x[...]


def body(queries, key, value, selection):
    me, side = lax.axis_index("ctx"), lax.axis_index("head")
    peers = lax.axis_size("ctx")
    fast, slow, order, groups = patterns(peers)
    steps = np.array([s for s, _ in order], np.int32)
    flips = np.array([f for _, f in order], np.int32)
    swap = [(0, 1), (1, 0)]
    okey, ovalue = lax.ppermute(key, "head", swap), lax.ppermute(value, "head", swap)

    picks = selection[:, :, 1:]
    asked = lax.dynamic_slice_in_dim(picks, side * KVG, KVG, 1)
    codes = (asked - 2 * me) * KVH + (side * KVG + jnp.arange(KVG, dtype=jnp.int32))[None, :, None] + 1
    wanted = jnp.max(
        jnp.where((asked >> 1) == me, codes, 0).reshape(peers, 2 * KVG * TOPK), axis=1
    )
    mine = lax.dynamic_slice_in_dim(picks, 2 * me + side, 1, 0)[0]
    owners = jnp.where(mine >= 0, mine >> 1, -1)
    local = jnp.any(owners == me, axis=1).astype(jnp.int32)
    s_from = me // fast - steps
    source = jnp.where(s_from >= 0, s_from * fast + ((me % fast) ^ flips), me)
    source = jnp.where(source < me, source, -2)
    heads = jnp.arange(KVH, dtype=jnp.int32)
    hit = jnp.any(owners[None, :, :] == source[:, None, None], axis=2)
    near = (heads // KVG) == side
    work_here = jnp.max(jnp.where(hit & near, heads, -1), axis=1)
    work_swap = jnp.max(jnp.where(hit & ~near, heads, -1), axis=1)
    meta = jnp.concatenate([jnp.stack([me, side]).astype(jnp.int32), wanted, local, work_here, work_swap])
    local_at = 2 + peers
    here_at = local_at + KVH
    swap_at = here_at + len(order)
    end = swap_at + len(order)

    piece_shape = jax.ShapeDtypeStruct((2 * BLK, HD), jnp.bfloat16)
    any_spec, vmem_spec = pl.BlockSpec(memory_space=ANY), pl.BlockSpec(memory_space=VMEM)
    sent = pl.pallas_call(
        functools.partial(cut_kernel, fast, slow, order),
        grid_spec=pltpu.PrefetchScalarGridSpec(
            num_scalar_prefetch=1,
            grid=(),
            in_specs=[vmem_spec] * 4,
            out_specs=[any_spec] * len(order),
            scratch_shapes=[pltpu.SemaphoreType.DMA((len(order), 2))],
        ),
        out_shape=[piece_shape] * len(order),
        cost_estimate=pl.CostEstimate(flops=0, bytes_accessed=len(order) << 19, transcendentals=0),
        name="cut",
    )(meta, key, value, okey, ovalue)
    sent = list(sent)

    state = (
        jax.ShapeDtypeStruct((KVH, GROUP, HD, BLK), jnp.float32),
        jax.ShapeDtypeStruct((KVH, 2 * GROUP, BLK), jnp.float32),
        jax.ShapeDtypeStruct((BLK, QH * HD), jnp.bfloat16),
    )
    kv_spec = pl.BlockSpec((BLK, HD), lambda g, _: (0, g))
    q_spec = pl.BlockSpec((BLK, WIDE), lambda g, _: (0, g))
    piece_flops = 4 * ROWS * BLK * HD
    acc, stat, out = pl.pallas_call(
        functools.partial(own_kernel, local_at),
        grid_spec=pltpu.PrefetchScalarGridSpec(
            num_scalar_prefetch=1,
            grid=(KVH,),
            in_specs=[q_spec] + [kv_spec] * 4,
            out_specs=[
                pl.BlockSpec((1, GROUP, HD, BLK), lambda g, _: (g, 0, 0, 0)),
                pl.BlockSpec((1, 2 * GROUP, BLK), lambda g, _: (g, 0, 0)),
                q_spec,
            ],
            scratch_shapes=[VMEM((HD, BLK), jnp.bfloat16)],
        ),
        out_shape=state,
        compiler_params=pltpu.CompilerParams(vmem_limit_bytes=52 << 20),
        cost_estimate=pl.CostEstimate(
            flops=32 * piece_flops, bytes_accessed=28 << 20, transcendentals=12 * ROWS * BLK
        ),
        name="own",
    )(meta, queries, key, value, okey, ovalue)

    landed = [None] * len(order)
    swapped = []

    def send(n):
        a, b = groups[n]
        for j in range(a, b):
            landed[j] = lax.ppermute(sent[j], "ctx", pairs_of(fast, slow, *order[j]))

    send(0)
    send(1)
    count = len(groups)
    for n in range(count + 1):
        a, b = groups[n] if n < count else (len(order), len(order))
        a0, b0 = groups[n - 1] if n else (0, 0)
        late = range(*groups[n + 2]) if n + 2 < count else range(0)
        n_here, n_pass = b - a, len(late)
        pieces = n_here + b0 - a0
        if n < count:
            parts = landed[a:b]
            joined, stat = pl.pallas_call(
                pack_kernel,
                in_specs=[vmem_spec] * n_here + [any_spec],
                out_specs=[vmem_spec, any_spec],
                out_shape=(jax.ShapeDtypeStruct((n_here * 2 * BLK, HD), jnp.bfloat16), state[1]),
                input_output_aliases={n_here: 1},
                compiler_params=pltpu.CompilerParams(vmem_limit_bytes=52 << 20),
                cost_estimate=pl.CostEstimate(flops=0, bytes_accessed=n_here << 19, transcendentals=0),
                name="pack",
            )(*parts, stat)
            swapped.append(lax.ppermute(joined, "head", swap))
        others = [swapped[n - 1]] if n else []
        base = 1 + n_here + len(others)
        result = pl.pallas_call(
            functools.partial(
                far_kernel, n_here, len(others), n_pass,
                here_at + a, (here_at + b, swap_at), swap_at + a0, (swap_at + b0, end),
            ),
            grid_spec=pltpu.PrefetchScalarGridSpec(
                num_scalar_prefetch=1,
                grid=(),
                in_specs=[any_spec] * (base - 1 + 4 + n_pass),
                out_specs=[any_spec] * (3 + n_pass),
                scratch_shapes=[
                    VMEM((KVH, BLK, WIDE), jnp.bfloat16),
                    VMEM((KVH, GROUP, HD, BLK), jnp.float32),
                    VMEM((KVH, 2 * GROUP, BLK), jnp.float32),
                    VMEM((KVH, BLK, WIDE), jnp.bfloat16),
                    VMEM((pieces, 2 * BLK, HD), jnp.bfloat16),
                    VMEM((HD, BLK), jnp.bfloat16),
                    pltpu.SMEM((KVH,), jnp.int32),
                    pltpu.SMEM((KVH,), jnp.int32),
                    pltpu.SMEM((KVH,), jnp.int32),
                    pltpu.SemaphoreType.DMA((pieces,)),
                    pltpu.SemaphoreType.DMA((KVH, 3)),
                    pltpu.SemaphoreType.DMA((KVH, 3)),
                ],
            ),
            out_shape=(*state, *[piece_shape] * n_pass),
            input_output_aliases={base + 1 + i: i for i in range(3 + n_pass)},
            compiler_params=pltpu.CompilerParams(vmem_limit_bytes=52 << 20),
            cost_estimate=pl.CostEstimate(
                flops=8 * pieces * piece_flops, bytes_accessed=pieces << 21, transcendentals=pieces * ROWS * BLK
            ),
            name="far",
        )(meta, *landed[a:b], *others, queries, acc, stat, out, *[sent[j] for j in late])
        acc, stat, out = result[:3]
        for j, x in zip(late, result[3:]):
            sent[j] = x
        if late:
            send(n + 2)
    return out


def solution(mesh):
    placed = (P(("ctx", "head"), None), P(("ctx", "head"), None), P(("ctx", "head"), None), P())
    return jax.shard_map(
        body, mesh=mesh, in_specs=placed, out_specs=P(("ctx", "head"), None), check_vma=False
    )
```

```python
import functools
import math

import jax
import jax.numpy as jnp
import numpy as np
from jax import lax
from jax.experimental import pallas as pl
from jax.experimental.pallas import tpu as pltpu
from jax.sharding import PartitionSpec as P

QH = 32
KVH = 8
HD = 128
BLK = 512
TOPK = 3
GROUP = QH // KVH
KVG = KVH // 2
WIDE = GROUP * HD
ROWS = GROUP * BLK
SCALE = math.log2(math.e) / math.sqrt(HD)
TILE = 128
VMEM = pltpu.VMEM
ANY = pl.ANY


def patterns(peers):
    fast = 4 if peers % 4 == 0 else 1
    slow = peers // fast

    def permute(moves, flip):
        pairs = [(a * fast + f, b * fast + (f ^ flip)) for a, b in moves for f in range(fast)]
        return [(a, b) for a, b in pairs if a < b]

    level = [(a, a) for a in range(slow)]
    if (fast, slow) == (4, 4):
        two, one, zero = [(0, 2), (1, 3)], [(0, 3), (1, 2)], [(0, 1), (2, 3)]
        order = []
        for m in range(3):
            order += [permute(two, m), permute(one, m), permute(zero, m)]
        order += [permute(level, 1), permute(two, 3), permute(level, 2), permute(level, 3), permute(zero, 3)]
        order += [permute(one, 3)]
        edges = [0, 3, 6, 10, 14, 15]
    else:
        order = []
        for m in range(fast):
            order += [permute([(a, a + d) for a in range(slow - d)], m) for d in range(1, slow)]
        order += [permute(level, m) for m in range(1, fast)]
        edges = [round(i * len(order) / 5) for i in range(6)]
    table = np.full((peers, 2 * len(order)), -2, np.int32)
    for n, pairs in enumerate(order):
        for a, b in pairs:
            table[a, n] = b
            table[b, len(order) + n] = a
    return order, table, list(zip(edges[:-1], edges[1:]))


def scores_of(k, q):
    return lax.dot_general(k, q, (((1,), (1,)), ((), ())), preferred_element_type=jnp.float32)


def total_of(vt, weights):
    return jnp.dot(vt, weights.astype(jnp.bfloat16), preferred_element_type=jnp.float32)


def cut_kernel(first, count, n_pass, meta, key, value, okey, ovalue, *rest):
    outs, sems = rest[n_pass : n_pass + count], rest[-1]
    side = meta[0]

    def each(act):
        for j in range(count):
            code = meta[1 + first + j] - 1
            block, head = code // KVH, code % KVH
            col = pl.multiple_of(jnp.maximum(head, 0) * HD, HD)
            for t, (here, there) in enumerate(((key, okey), (value, ovalue))):
                to = outs[j].at[pl.ds(t * BLK, BLK), :]
                mine = pltpu.make_async_copy(here.at[:, pl.ds(col, HD)], to, sems.at[j, t])
                other = pltpu.make_async_copy(there.at[:, pl.ds(col, HD)], to, sems.at[j, t])
                act(jnp.logical_and(code >= 0, block == side), mine)
                act(jnp.logical_and(code >= 0, block != side), other)

    def start(flag, copy):
        pl.when(flag)(copy.start)

    def wait(flag, copy):
        pl.when(flag)(copy.wait)

    each(start)
    each(wait)


def own_kernel(local_at, work, meta, q, k, v, ok, ov, acc_out, stat_out, out, vt, outs, uses, sem):
    g = pl.program_id(0)
    cols = pl.ds(pl.multiple_of(g * HD, HD), HD)
    vt[...] = v[:, cols].T
    low = lax.broadcasted_iota(jnp.int32, (TILE, TILE), 1) >= lax.broadcasted_iota(jnp.int32, (TILE, TILE), 0)
    for r in reversed(range(BLK // TILE)):
        keys, at = (r + 1) * TILE, slice(r * TILE, (r + 1) * TILE)
        for j in range(GROUP):
            scores = scores_of(k[:keys, cols], q[at, j * HD : (j + 1) * HD])
            last = jnp.where(low, scores[r * TILE :], -1e30)
            scores = jnp.concatenate([scores[: r * TILE], last], axis=0) if r else last
            m = jnp.max(scores, axis=0, keepdims=True)
            weights = jnp.exp2((scores - m) * SCALE)
            stat_out[0, j : j + 1, at] = m
            stat_out[0, GROUP + j : GROUP + j + 1, at] = jnp.sum(weights, axis=0, keepdims=True)
            acc_out[0, j, :, at] = total_of(vt[:, :keys], weights)

    @pl.when(meta[local_at + g] > 0)
    def _():
        vt[...] = ov[:, cols].T
        fold(ok.at[:, cols], lambda at, col: q[at, col], vt, acc_out.at[0], stat_out.at[0])

    uses[0] = 0

    def count(i, carry):
        uses[0] = uses[0] + jnp.where(meta[i] == g, 1, 0)
        return carry

    lax.fori_loop(*work, count, 0)

    @pl.when(uses[0] == 0)
    def _():
        for j in range(GROUP):
            total = stat_out[0, GROUP + j : GROUP + j + 1, :]
            outs[:, j * HD : (j + 1) * HD] = (acc_out[0, j] / total).astype(jnp.bfloat16).T
        copy = pltpu.make_async_copy(outs, out.at[:, pl.ds(pl.multiple_of(g * WIDE, WIDE), WIDE)], sem)
        copy.start()
        copy.wait()


def fold(k, q_of, vt, acc, stat):
    for j in range(GROUP):
        for r in range(BLK // TILE):
            at = slice(r * TILE, (r + 1) * TILE)
            scores = scores_of(k[...], q_of(at, slice(j * HD, (j + 1) * HD)))
            m_old = stat[j : j + 1, at]
            m = jnp.maximum(m_old, jnp.max(scores, axis=0, keepdims=True))
            weights = jnp.exp2((scores - m) * SCALE)
            alpha = jnp.exp2((m_old - m) * SCALE)
            total = GROUP + j
            stat[j : j + 1, at] = m
            stat[total : total + 1, at] = stat[total : total + 1, at] * alpha + jnp.sum(weights, axis=0, keepdims=True)
            acc[j, :, at] = acc[j, :, at] * alpha + total_of(vt[...], weights)


def far_kernel(n_here, n_swap, here_at, here_later, swap_at, swap_later, meta, *refs):
    arrived, refs = refs[:n_here], refs[n_here:]
    swapped, refs = refs[:n_swap], refs[n_swap:]
    q_hbm, acc_hbm, stat_hbm = refs[:3]
    refs = refs[4:]
    acc_new, stat_new, out_new = refs[:3]
    qs, accs, stats, outs, kv, vt, seen, here, later, kv_sem, in_sem, out_sem = refs[3:]
    each = n_swap and swapped[0].shape[0] // (2 * BLK)
    pieces = n_here + n_swap * each

    def wide(g):
        return pl.ds(pl.multiple_of(g * WIDE, WIDE), WIDE)

    def loads(g):
        return (
            pltpu.make_async_copy(q_hbm.at[:, wide(g)], qs.at[g], in_sem.at[g, 0]),
            pltpu.make_async_copy(acc_hbm.at[g], accs.at[g], in_sem.at[g, 1]),
            pltpu.make_async_copy(stat_hbm.at[g], stats.at[g], in_sem.at[g, 2]),
        )

    def stores(g):
        return (
            pltpu.make_async_copy(accs.at[g], acc_new.at[g], out_sem.at[g, 0]),
            pltpu.make_async_copy(stats.at[g], stat_new.at[g], out_sem.at[g, 1]),
        )

    def finish(g):
        return pltpu.make_async_copy(outs.at[g], out_new.at[:, wide(g)], out_sem.at[g, 2])

    def head_of(i):
        return meta[jnp.where(i < n_here, here_at + i, swap_at + i - n_here)]

    for g in range(KVH):
        seen[g] = 0
        here[g] = 0
        later[g] = 0

    for i in range(pieces):
        g = meta[here_at + i] if i < n_here else meta[swap_at + i - n_here]
        block = arrived[i] if i < n_here else swapped[0].at[pl.ds((i - n_here) * 2 * BLK, 2 * BLK), :]

        @pl.when(g >= 0)
        def _():
            pltpu.make_async_copy(block, kv.at[i], kv_sem.at[i]).start()

            @pl.when(here[g] == 0)
            def _():
                for copy in loads(g):
                    copy.start()

            here[g] = here[g] + 1

    def count(i, carry):
        g = meta[i]

        @pl.when(g >= 0)
        def _():
            later[g] = later[g] + 1

        return carry

    lax.fori_loop(*here_later, count, 0)
    lax.fori_loop(*swap_later, count, 0)

    def piece(i, carry):
        g = head_of(i)

        @pl.when(g >= 0)
        def _():
            @pl.when(seen[g] == 0)
            def _():
                for copy in loads(g):
                    copy.wait()

            pltpu.make_async_copy(kv.at[i], kv.at[i], kv_sem.at[i]).wait()
            vt[...] = kv[i, BLK:, :].T
            fold(
                kv.at[i, pl.ds(0, BLK), :], lambda at, col: qs[g, at, col], vt, accs.at[g], stats.at[g]
            )
            seen[g] = seen[g] + 1
            done = seen[g] == here[g]

            @pl.when(jnp.logical_and(done, later[g] > 0))
            def _():
                for copy in stores(g):
                    copy.start()

            @pl.when(jnp.logical_and(done, later[g] == 0))
            def _():
                for j in range(GROUP):
                    outs[g, :, j * HD : (j + 1) * HD] = (
                        (accs[g, j] / stats[g, GROUP + j : GROUP + j + 1, :]).astype(jnp.bfloat16).T
                    )
                finish(g).start()

        return carry

    lax.fori_loop(0, pieces, piece, 0)

    for g in range(KVH):
        used = here[g] > 0

        @pl.when(jnp.logical_and(used, later[g] > 0))
        def _():
            for copy in stores(g):
                copy.wait()

        @pl.when(jnp.logical_and(used, later[g] == 0))
        def _():
            finish(g).wait()


def pack_kernel(count, n_pass, *refs):
    joined = refs[count + 1 + n_pass]
    for i in range(count):
        joined[i * 2 * BLK : (i + 1) * 2 * BLK, :] = refs[i][...]


def body(queries, key, value, selection):
    me, side = lax.axis_index("ctx"), lax.axis_index("head")
    peers = lax.axis_size("ctx")
    order, table, groups = patterns(peers)
    total = len(order)
    swap = [(0, 1), (1, 0)]
    okey, ovalue = lax.ppermute(key, "head", swap), lax.ppermute(value, "head", swap)

    ends = lax.dynamic_index_in_dim(jnp.asarray(table), me, 0, keepdims=False)
    targets, sources = ends[:total], ends[total:]
    picks = selection[:, :, 1:]
    asked = lax.dynamic_slice_in_dim(picks, side * KVG, KVG, 1)
    codes = (asked - 2 * me) * KVH + (side * KVG + jnp.arange(KVG, dtype=jnp.int32))[None, :, None] + 1
    wanted = jnp.max(
        jnp.where((asked >> 1) == me, codes, 0).reshape(peers, 2 * KVG * TOPK), axis=1
    )
    cuts = jnp.max(
        jnp.where(targets[:, None] == jnp.arange(peers, dtype=jnp.int32)[None, :], wanted[None, :], 0), axis=1
    )
    mine = lax.dynamic_slice_in_dim(picks, 2 * me + side, 1, 0)[0]
    owners = jnp.where(mine >= 0, mine >> 1, -1)
    local = jnp.any(owners == me, axis=1).astype(jnp.int32)
    heads = jnp.arange(KVH, dtype=jnp.int32)
    hit = jnp.any(owners[None, :, :] == sources[:, None, None], axis=2)
    near = (heads // KVG) == side
    work_here = jnp.max(jnp.where(hit & near, heads, -1), axis=1)
    work_swap = jnp.max(jnp.where(hit & ~near, heads, -1), axis=1)
    meta = jnp.concatenate([side[None].astype(jnp.int32), cuts, local, work_here, work_swap])
    local_at = 1 + total
    here_at = local_at + KVH
    swap_at = here_at + total
    end = swap_at + total

    piece_shape = jax.ShapeDtypeStruct((2 * BLK, HD), jnp.bfloat16)
    any_spec, vmem_spec = pl.BlockSpec(memory_space=ANY), pl.BlockSpec(memory_space=VMEM)
    state = (
        jax.ShapeDtypeStruct((KVH, GROUP, HD, BLK), jnp.float32),
        jax.ShapeDtypeStruct((KVH, 2 * GROUP, BLK), jnp.float32),
        jax.ShapeDtypeStruct((BLK, QH * HD), jnp.bfloat16),
    )
    params = pltpu.CompilerParams(vmem_limit_bytes=48 << 20)

    def cut(first, last, *through):
        count = last - first
        return pl.pallas_call(
            functools.partial(cut_kernel, first, count, len(through)),
            grid_spec=pltpu.PrefetchScalarGridSpec(
                num_scalar_prefetch=1,
                grid=(),
                in_specs=[vmem_spec] * 4 + [any_spec] * len(through),
                out_specs=[any_spec] * (count + len(through)),
                scratch_shapes=[pltpu.SemaphoreType.DMA((count, 2))],
            ),
            out_shape=[piece_shape] * count + [jax.ShapeDtypeStruct(x.shape, x.dtype) for x in through],
            input_output_aliases={5 + i: count + i for i in range(len(through))},
            cost_estimate=pl.CostEstimate(flops=0, bytes_accessed=count << 19, transcendentals=0),
            name="cut",
        )(meta, key, value, okey, ovalue, *through)

    early = min(5, groups[1][1])
    sent = list(cut(0, early))

    q_spec = pl.BlockSpec((BLK, WIDE), lambda g, _: (0, g))
    piece_flops = 4 * ROWS * BLK * HD
    acc, stat, out = pl.pallas_call(
        functools.partial(own_kernel, local_at, (here_at, end)),
        grid_spec=pltpu.PrefetchScalarGridSpec(
            num_scalar_prefetch=1,
            grid=(KVH,),
            in_specs=[q_spec] + [vmem_spec] * 4,
            out_specs=[
                pl.BlockSpec((1, GROUP, HD, BLK), lambda g, _: (g, 0, 0, 0)),
                pl.BlockSpec((1, 2 * GROUP, BLK), lambda g, _: (g, 0, 0)),
                any_spec,
            ],
            scratch_shapes=[
                VMEM((HD, BLK), jnp.bfloat16),
                VMEM((BLK, WIDE), jnp.bfloat16),
                pltpu.SMEM((1,), jnp.int32),
                pltpu.SemaphoreType.DMA,
            ],
        ),
        out_shape=state,
        compiler_params=params,
        cost_estimate=pl.CostEstimate(
            flops=32 * piece_flops, bytes_accessed=28 << 20, transcendentals=12 * ROWS * BLK
        ),
        name="own",
    )(meta, queries, key, value, okey, ovalue)
    *rest, stat = cut(early, total, stat)
    sent += rest

    landed = [None] * total
    swapped = []

    def send(n):
        a, b = groups[n]
        for j in range(a, b):
            landed[j] = lax.ppermute(sent[j], "ctx", order[j])

    def pack(n, stat):
        a, b = groups[n]
        late = list(range(*groups[n + 2])) if n + 2 < len(groups) else []
        count = b - a
        joined, stat, *through = pl.pallas_call(
            functools.partial(pack_kernel, count, len(late)),
            in_specs=[vmem_spec] * count + [any_spec] * (1 + len(late)),
            out_specs=[vmem_spec] + [any_spec] * (1 + len(late)),
            out_shape=(jax.ShapeDtypeStruct((count * 2 * BLK, HD), jnp.bfloat16), state[1], *[piece_shape] * len(late)),
            input_output_aliases={count + i: 1 + i for i in range(1 + len(late))},
            compiler_params=params,
            cost_estimate=pl.CostEstimate(flops=0, bytes_accessed=count << 19, transcendentals=0),
            name="pack",
        )(*landed[a:b], stat, *[sent[j] for j in late])
        swapped.append(lax.ppermute(joined, "head", swap))
        for j, x in zip(late, through):
            sent[j] = x
        if late:
            send(n + 2)
        return stat

    def far(here, swaps, acc, stat, out):
        a, b = groups[here] if here is not None else (0, 0)
        a0, b0 = groups[swaps] if swaps is not None else (0, 0)
        here_end = max(b, b0)
        swap_end = b0 if swaps is not None else (groups[here - 1][1] if here else 0)
        n_here = b - a
        pieces = n_here + b0 - a0
        others = [swapped[swaps]] if swaps is not None else []
        base = 1 + n_here + len(others)
        return pl.pallas_call(
            functools.partial(
                far_kernel, n_here, len(others),
                here_at + a, (here_at + here_end, swap_at), swap_at + a0, (swap_at + swap_end, end),
            ),
            grid_spec=pltpu.PrefetchScalarGridSpec(
                num_scalar_prefetch=1,
                grid=(),
                in_specs=[any_spec] * (base - 1 + 4),
                out_specs=[any_spec] * 3,
                scratch_shapes=[
                    VMEM((KVH, BLK, WIDE), jnp.bfloat16),
                    VMEM((KVH, GROUP, HD, BLK), jnp.float32),
                    VMEM((KVH, 2 * GROUP, BLK), jnp.float32),
                    VMEM((KVH, BLK, WIDE), jnp.bfloat16),
                    VMEM((pieces, 2 * BLK, HD), jnp.bfloat16),
                    VMEM((HD, BLK), jnp.bfloat16),
                    pltpu.SMEM((KVH,), jnp.int32),
                    pltpu.SMEM((KVH,), jnp.int32),
                    pltpu.SMEM((KVH,), jnp.int32),
                    pltpu.SemaphoreType.DMA((pieces,)),
                    pltpu.SemaphoreType.DMA((KVH, 3)),
                    pltpu.SemaphoreType.DMA((KVH, 3)),
                ],
            ),
            out_shape=state,
            input_output_aliases={base + 1 + i: i for i in range(3)},
            compiler_params=params,
            cost_estimate=pl.CostEstimate(
                flops=8 * pieces * piece_flops, bytes_accessed=pieces << 21, transcendentals=pieces * ROWS * BLK
            ),
            name="far",
        )(meta, *landed[a:b], *others, queries, acc, stat, out)

    send(0)
    send(1)
    last = len(groups) - 1
    for n in range(last):
        stat = pack(n, stat)
        acc, stat, out = far(n, n - 1 if n else None, acc, stat, out)
    acc, stat, out = far(None, last - 1, acc, stat, out)
    stat = pack(last, stat)
    acc, stat, out = far(last, None, acc, stat, out)
    acc, stat, out = far(None, last, acc, stat, out)
    return out


def solution(mesh):
    placed = (P(("ctx", "head"), None), P(("ctx", "head"), None), P(("ctx", "head"), None), P())
    return jax.shard_map(
        body, mesh=mesh, in_specs=placed, out_specs=P(("ctx", "head"), None), check_vma=False
    )
```

```python
import functools
import math

import jax
import jax.numpy as jnp
import numpy as np
from jax import lax
from jax.experimental import pallas as pl
from jax.experimental.pallas import tpu as pltpu
from jax.sharding import PartitionSpec as P

QH = 32
KVH = 8
HD = 128
BLK = 512
TOPK = 3
GROUP = QH // KVH
KVG = KVH // 2
WIDE = GROUP * HD
ROWS = GROUP * BLK
SCALE = math.log2(math.e) / math.sqrt(HD)
TILE = 128
VMEM = pltpu.VMEM
ANY = pl.ANY


def patterns(peers):
    fast = 4 if peers % 4 == 0 else 1
    slow = peers // fast

    def permute(moves, flip):
        pairs = [(a * fast + f, b * fast + (f ^ flip)) for a, b in moves for f in range(fast)]
        return [(a, b) for a, b in pairs if a < b]

    level = [(a, a) for a in range(slow)]
    if (fast, slow) == (4, 4):
        two, one, zero = [(0, 2), (1, 3)], [(0, 3), (1, 2)], [(0, 1), (2, 3)]
        order = []
        for m in range(3):
            order += [permute(two, m), permute(one, m), permute(zero, m)]
        order += [permute(level, 1), permute(two, 3), permute(level, 2), permute(level, 3), permute(zero, 3)]
        order += [permute(one, 3)]
        edges = [0, 3, 6, 10, 14, 15]
    else:
        order = []
        for m in range(fast):
            order += [permute([(a, a + d) for a in range(slow - d)], m) for d in range(1, slow)]
        order += [permute(level, m) for m in range(1, fast)]
        edges = [round(i * len(order) / 5) for i in range(6)]
    table = np.full((peers, 2 * len(order)), -2, np.int32)
    for n, pairs in enumerate(order):
        for a, b in pairs:
            table[a, n] = b
            table[b, len(order) + n] = a
    return order, table, list(zip(edges[:-1], edges[1:]))


def scores_of(k, q):
    return lax.dot_general(k, q, (((1,), (1,)), ((), ())), preferred_element_type=jnp.float32)


def total_of(vt, weights):
    return jnp.dot(vt, weights.astype(jnp.bfloat16), preferred_element_type=jnp.float32)


def cut_kernel(count, meta, key, value, okey, ovalue, *rest):
    outs, sems = rest[:-1], rest[-1]
    side = meta[0]

    def each(act):
        for j in range(count):
            code = meta[1 + j] - 1
            block, head = code // KVH, code % KVH
            col = pl.multiple_of(jnp.maximum(head, 0) * HD, HD)
            for t, (here, there) in enumerate(((key, okey), (value, ovalue))):
                to = outs[j].at[pl.ds(t * BLK, BLK), :]
                mine = pltpu.make_async_copy(here.at[:, pl.ds(col, HD)], to, sems.at[j, t])
                other = pltpu.make_async_copy(there.at[:, pl.ds(col, HD)], to, sems.at[j, t])
                act(jnp.logical_and(code >= 0, block == side), mine)
                act(jnp.logical_and(code >= 0, block != side), other)

    def start(flag, copy):
        pl.when(flag)(copy.start)

    def wait(flag, copy):
        pl.when(flag)(copy.wait)

    each(start)
    each(wait)


def own_kernel(local_at, work, meta, q, k, v, ok, ov, acc_out, stat_out, out, vt, outs, later, sems):
    low = lax.broadcasted_iota(jnp.int32, (TILE, TILE), 1) >= lax.broadcasted_iota(jnp.int32, (TILE, TILE), 0)
    count_heads(meta, later, work)

    def finish(g):
        return pltpu.make_async_copy(outs.at[g], out.at[:, wide(g)], sems.at[g])

    def head(g, carry):
        cols = pl.ds(pl.multiple_of(g * HD, HD), HD)
        vt[...] = v[:, cols].T
        for r in reversed(range(BLK // TILE)):
            keys, at = (r + 1) * TILE, slice(r * TILE, (r + 1) * TILE)
            for j in range(GROUP):
                scores = scores_of(k[:keys, cols], q[at, part(g, j)])
                last = jnp.where(low, scores[r * TILE :], -1e30)
                scores = jnp.concatenate([scores[: r * TILE], last], axis=0) if r else last
                m = jnp.max(scores, axis=0, keepdims=True)
                weights = jnp.exp2((scores - m) * SCALE)
                stat_out[g, j : j + 1, at] = m
                stat_out[g, GROUP + j : GROUP + j + 1, at] = jnp.sum(weights, axis=0, keepdims=True)
                acc_out[g, j, :, at] = total_of(vt[:, :keys], weights)

        @pl.when(meta[local_at + g] > 0)
        def _():
            vt[...] = ov[:, cols].T
            fold(g, q, ok.at[:, cols], vt, acc_out, stat_out, acc_out, stat_out)

        @pl.when(later[g] == 0)
        def _():
            write_out(g, acc_out, stat_out, outs)
            finish(g).start()

        return carry

    lax.fori_loop(0, KVH, head, 0)
    for g in range(KVH):
        pl.when(later[g] == 0)(finish(g).wait)


def wide(g):
    return pl.ds(pl.multiple_of(g * WIDE, WIDE), WIDE)


def part(g, j):
    return pl.ds(pl.multiple_of(g * WIDE + j * HD, HD), HD)


def count_heads(meta, counts, *spans):
    for g in range(KVH):
        counts[g] = 0

    def count(i, carry):
        g = meta[i]

        @pl.when(g >= 0)
        def _():
            counts[g] = counts[g] + 1

        return carry

    for span in spans:
        lax.fori_loop(*span, count, 0)


def write_out(g, acc, stat, outs):
    for j in range(GROUP):
        total = stat[g, GROUP + j : GROUP + j + 1, :]
        outs[g, :, j * HD : (j + 1) * HD] = (acc[g, j] / total).astype(jnp.bfloat16).T


def fold(g, q, k, vt, acc, stat, acc_out, stat_out):
    for j in range(GROUP):
        for r in range(BLK // TILE):
            at, total = slice(r * TILE, (r + 1) * TILE), GROUP + j
            scores = scores_of(k[...], q[at, part(g, j)])
            m_old = stat[g, j : j + 1, at]
            m = jnp.maximum(m_old, jnp.max(scores, axis=0, keepdims=True))
            weights = jnp.exp2((scores - m) * SCALE)
            alpha = jnp.exp2((m_old - m) * SCALE)
            sums = stat[g, total : total + 1, at] * alpha + jnp.sum(weights, axis=0, keepdims=True)
            stat_out[g, j : j + 1, at] = m
            stat_out[g, total : total + 1, at] = sums
            acc_out[g, j, :, at] = acc[g, j, :, at] * alpha + total_of(vt[...], weights)


def far_kernel(n_here, n_swap, here_at, here_later, swap_at, swap_later, meta, *refs):
    arrived, refs = refs[:n_here], refs[n_here:]
    swapped, refs = refs[:n_swap], refs[n_swap:]
    q, acc, stat, _, acc_out, stat_out, out, outs, kv, vt, seen, here, later, kv_sem, out_sem = refs
    pieces = n_here + (swapped[0].shape[0] // (2 * BLK) if n_swap else 0)

    def finish(g):
        return pltpu.make_async_copy(outs.at[g], out.at[:, wide(g)], out_sem.at[g])

    for i in range(pieces):
        g = meta[here_at + i] if i < n_here else meta[swap_at + i - n_here]
        block = arrived[i] if i < n_here else swapped[0].at[pl.ds((i - n_here) * 2 * BLK, 2 * BLK), :]
        pl.when(g >= 0)(pltpu.make_async_copy(block, kv.at[i], kv_sem.at[i]).start)

    count_heads(meta, here, (here_at, here_at + n_here), (swap_at, swap_at + pieces - n_here))
    count_heads(meta, later, here_later, swap_later)
    for g in range(KVH):
        seen[g] = 0

        @pl.when(jnp.logical_and(later[g] > 0, here[g] == 0))
        def _():
            acc_out[g] = acc[g]
            stat_out[g] = stat[g]

    def piece(i, carry):
        g = meta[jnp.where(i < n_here, here_at + i, swap_at + i - n_here)]

        @pl.when(g >= 0)
        def _():
            @pl.when(seen[g] == 0)
            def _():
                acc_out[g] = acc[g]
                stat_out[g] = stat[g]

            pltpu.make_async_copy(kv.at[i], kv.at[i], kv_sem.at[i]).wait()
            vt[...] = kv[i, BLK:, :].T
            fold(g, q, kv.at[i, pl.ds(0, BLK), :], vt, acc_out, stat_out, acc_out, stat_out)
            seen[g] = seen[g] + 1

            @pl.when(jnp.logical_and(seen[g] == here[g], later[g] == 0))
            def _():
                write_out(g, acc_out, stat_out, outs)
                finish(g).start()

        return carry

    lax.fori_loop(0, pieces, piece, 0)
    for g in range(KVH):
        pl.when(jnp.logical_and(here[g] > 0, later[g] == 0))(finish(g).wait)


def pack_kernel(count, *refs):
    joined = refs[count + 1]
    for i in range(count):
        joined[i * 2 * BLK : (i + 1) * 2 * BLK, :] = refs[i][...]
    refs[count + 2][...] = refs[count][...]


def body(queries, key, value, selection):
    me, side = lax.axis_index("ctx"), lax.axis_index("head")
    peers = lax.axis_size("ctx")
    order, table, groups = patterns(peers)
    total = len(order)
    swap = [(0, 1), (1, 0)]
    okey, ovalue = lax.ppermute(key, "head", swap), lax.ppermute(value, "head", swap)

    ends = lax.dynamic_index_in_dim(jnp.asarray(table), me, 0, keepdims=False)
    targets, sources = ends[:total], ends[total:]
    picks = selection[:, :, 1:]
    asked = lax.dynamic_slice_in_dim(picks, side * KVG, KVG, 1)
    codes = (asked - 2 * me) * KVH + (side * KVG + jnp.arange(KVG, dtype=jnp.int32))[None, :, None] + 1
    wanted = jnp.max(
        jnp.where((asked >> 1) == me, codes, 0).reshape(peers, 2 * KVG * TOPK), axis=1
    )
    cuts = jnp.max(
        jnp.where(targets[:, None] == jnp.arange(peers, dtype=jnp.int32)[None, :], wanted[None, :], 0), axis=1
    )
    mine = lax.dynamic_slice_in_dim(picks, 2 * me + side, 1, 0)[0]
    owners = jnp.where(mine >= 0, mine >> 1, -1)
    local = jnp.any(owners == me, axis=1).astype(jnp.int32)
    heads = jnp.arange(KVH, dtype=jnp.int32)
    hit = jnp.any(owners[None, :, :] == sources[:, None, None], axis=2)
    near = (heads // KVG) == side
    work_here = jnp.max(jnp.where(hit & near, heads, -1), axis=1)
    work_swap = jnp.max(jnp.where(hit & ~near, heads, -1), axis=1)
    meta = jnp.concatenate([side[None].astype(jnp.int32), cuts, local, work_here, work_swap])
    local_at = 1 + total
    here_at = local_at + KVH
    swap_at = here_at + total
    end = swap_at + total

    piece_shape = jax.ShapeDtypeStruct((2 * BLK, HD), jnp.bfloat16)
    any_spec, vmem_spec = pl.BlockSpec(memory_space=ANY), pl.BlockSpec(memory_space=VMEM)
    state = (
        jax.ShapeDtypeStruct((KVH, GROUP, HD, BLK), jnp.float32),
        jax.ShapeDtypeStruct((KVH, 2 * GROUP, BLK), jnp.float32),
        jax.ShapeDtypeStruct((BLK, QH * HD), jnp.bfloat16),
    )
    params = pltpu.CompilerParams(vmem_limit_bytes=16 << 20)

    sent = pl.pallas_call(
        functools.partial(cut_kernel, total),
        grid_spec=pltpu.PrefetchScalarGridSpec(
            num_scalar_prefetch=1,
            grid=(),
            in_specs=[vmem_spec] * 4,
            out_specs=[any_spec] * total,
            scratch_shapes=[pltpu.SemaphoreType.DMA((total, 2))],
        ),
        out_shape=[piece_shape] * total,
        compiler_params=params,
        cost_estimate=pl.CostEstimate(flops=0, bytes_accessed=total << 19, transcendentals=0),
        name="cut",
    )(meta, key, value, okey, ovalue)

    piece_flops = 4 * ROWS * BLK * HD
    acc, stat, out = pl.pallas_call(
        functools.partial(own_kernel, local_at, (here_at, end)),
        grid_spec=pltpu.PrefetchScalarGridSpec(
            num_scalar_prefetch=1,
            grid=(),
            in_specs=[vmem_spec] * 5,
            out_specs=[vmem_spec, vmem_spec, any_spec],
            scratch_shapes=[
                VMEM((HD, BLK), jnp.bfloat16),
                VMEM((KVH, BLK, WIDE), jnp.bfloat16),
                pltpu.SMEM((KVH,), jnp.int32),
                pltpu.SemaphoreType.DMA((KVH,)),
            ],
        ),
        out_shape=state,
        compiler_params=params,
        cost_estimate=pl.CostEstimate(
            flops=32 * piece_flops, bytes_accessed=28 << 20, transcendentals=12 * ROWS * BLK
        ),
        name="own",
    )(meta, queries, key, value, okey, ovalue)

    landed = [None] * total
    swapped = []

    def send(n):
        a, b = groups[n]
        for j in range(a, b):
            landed[j] = lax.ppermute(sent[j], "ctx", order[j])

    def pack(n, stat):
        a, b = groups[n]
        count = b - a
        joined, stat = pl.pallas_call(
            functools.partial(pack_kernel, count),
            in_specs=[vmem_spec] * (count + 1),
            out_specs=[vmem_spec] * 2,
            out_shape=(jax.ShapeDtypeStruct((count * 2 * BLK, HD), jnp.bfloat16), state[1]),
            input_output_aliases={count: 1},
            compiler_params=params,
            cost_estimate=pl.CostEstimate(flops=0, bytes_accessed=count << 19, transcendentals=0),
            name="pack",
        )(*landed[a:b], stat)
        swapped.append(lax.ppermute(joined, "head", swap))
        return stat

    def far(here, swaps, acc, stat, out):
        a, b = groups[here] if here is not None else (0, 0)
        a0, b0 = groups[swaps] if swaps is not None else (0, 0)
        here_end = max(b, b0)
        swap_end = b0 if swaps is not None else (groups[here - 1][1] if here else 0)
        n_here = b - a
        pieces = n_here + b0 - a0
        others = [swapped[swaps]] if swaps is not None else []
        base = 1 + n_here + len(others)
        return pl.pallas_call(
            functools.partial(
                far_kernel, n_here, len(others),
                here_at + a, (here_at + here_end, swap_at), swap_at + a0, (swap_at + swap_end, end),
            ),
            grid_spec=pltpu.PrefetchScalarGridSpec(
                num_scalar_prefetch=1,
                grid=(),
                in_specs=[any_spec] * (base - 1) + [vmem_spec] * 3 + [any_spec],
                out_specs=[vmem_spec, vmem_spec, any_spec],
                scratch_shapes=[
                    VMEM((KVH, BLK, WIDE), jnp.bfloat16),
                    VMEM((pieces, 2 * BLK, HD), jnp.bfloat16),
                    VMEM((HD, BLK), jnp.bfloat16),
                    pltpu.SMEM((KVH,), jnp.int32),
                    pltpu.SMEM((KVH,), jnp.int32),
                    pltpu.SMEM((KVH,), jnp.int32),
                    pltpu.SemaphoreType.DMA((pieces,)),
                    pltpu.SemaphoreType.DMA((KVH,)),
                ],
            ),
            out_shape=state,
            input_output_aliases={base + 1 + i: i for i in range(3)},
            compiler_params=params,
            cost_estimate=pl.CostEstimate(
                flops=8 * pieces * piece_flops, bytes_accessed=pieces << 21, transcendentals=pieces * ROWS * BLK
            ),
            name="far",
        )(meta, *landed[a:b], *others, queries, acc, stat, out)

    for n in range(len(groups)):
        send(n)
    last = len(groups) - 1
    for n in range(last):
        stat = pack(n, stat)
        acc, stat, out = far(n, n - 1 if n else None, acc, stat, out)
    acc, stat, out = far(None, last - 1, acc, stat, out)
    stat = pack(last, stat)
    acc, stat, out = far(last, None, acc, stat, out)
    acc, stat, out = far(None, last, acc, stat, out)
    return out


def solution(mesh):
    placed = (P(("ctx", "head"), None), P(("ctx", "head"), None), P(("ctx", "head"), None), P())
    return jax.shard_map(
        body, mesh=mesh, in_specs=placed, out_specs=P(("ctx", "head"), None), check_vma=False
    )
```

```python
import functools
import math

import jax
import jax.numpy as jnp
import numpy as np
from jax import lax
from jax.experimental import pallas as pl
from jax.experimental.pallas import tpu as pltpu
from jax.sharding import PartitionSpec as P

QH = 32
KVH = 8
HD = 128
BLK = 512
TOPK = 3
GROUP = QH // KVH
KVG = KVH // 2
WIDE = GROUP * HD
ROWS = GROUP * BLK
SCALE = math.log2(math.e) / math.sqrt(HD)
TILE = 128
SPAN = 256
ALL_TILES = [
    (j, r, lo, lo + SPAN, False, False) for lo in range(0, BLK, SPAN) for j in range(GROUP) for r in range(BLK // TILE)
]
VMEM = pltpu.VMEM
ANY = pl.ANY


def patterns(peers):
    fast = 4 if peers % 4 == 0 else 1
    slow = peers // fast

    def permute(moves, flip):
        pairs = [(a * fast + f, b * fast + (f ^ flip)) for a, b in moves for f in range(fast)]
        return [(a, b) for a, b in pairs if a < b]

    level = [(a, a) for a in range(slow)]
    if (fast, slow) == (4, 4):
        two, one, zero = [(0, 2), (1, 3)], [(0, 3), (1, 2)], [(0, 1), (2, 3)]
        order = [permute(two, 0), permute(one, 0), permute(level, 1)]
        order += [permute(two, 1), permute(one, 1), permute(zero, 0)]
        order += [permute(two, 2), permute(one, 2), permute(zero, 1), permute(level, 2)]
        order += [permute(two, 3), permute(zero, 2), permute(level, 3), permute(zero, 3)]
        order += [permute(one, 3)]
        edges = [0, 3, 6, 10, 14, 15]
    else:
        order = []
        for m in range(fast):
            order += [permute([(a, a + d) for a in range(slow - d)], m) for d in range(1, slow)]
        order += [permute(level, m) for m in range(1, fast)]
        edges = [round(i * len(order) / 5) for i in range(6)]
    table = np.full((peers, 2 * len(order)), -2, np.int32)
    for n, pairs in enumerate(order):
        for a, b in pairs:
            table[a, n] = b
            table[b, len(order) + n] = a
    return order, table, list(zip(edges[:-1], edges[1:]))


def scores_of(k, q):
    return lax.dot_general(k, q, (((1,), (1,)), ((), ())), preferred_element_type=jnp.float32)


def total_of(vt, weights):
    return jnp.dot(vt, weights.astype(jnp.bfloat16), preferred_element_type=jnp.float32)


def cut_copies(act, own, first, meta, key, value, okey, ovalue, outs, sems):
    for j, to in enumerate(outs):
        code = meta[1 + first + j] - 1
        block, head = code // KVH, code % KVH
        col = pl.ds(pl.multiple_of(jnp.maximum(head, 0) * HD, HD), HD)
        flag = jnp.logical_and(code >= 0, (block == meta[0]) if own else (block != meta[0]))
        for t, source in enumerate((key, value) if own else (okey, ovalue)):
            copy = pltpu.make_async_copy(source.at[:, col], to.at[pl.ds(t * BLK, BLK), :], sems.at[j, t])
            pl.when(flag)(copy.start if act == "start" else copy.wait)


def cut_kernel(meta, key, value, okey, ovalue, *rest):
    outs, sems = rest[:-1], rest[-1]
    args = (0, meta, key, value, okey, ovalue, outs, sems)
    for act in ("start", "wait"):
        for own in (False, True):
            cut_copies(act, own, *args)


def own_kernel(local_at, work, first, meta, q, k, v, ok, ov, acc_out, stat_out, out, *rest):
    sent, (vt, outs, later, sems, cut_sems) = rest[:-5], rest[-5:]
    args = (first, meta, k, v, ok, ov, sent, cut_sems)
    for own in (False, True):
        cut_copies("start", own, *args)
    count_heads(meta, later, work)
    for g in range(KVH):
        later[g] = later[g] + meta[local_at + g]
    tiles = []
    for lo in range(0, BLK, SPAN):
        for j in range(GROUP):
            for r in range(lo // TILE, BLK // TILE):
                hi = min(lo + SPAN, (r + 1) * TILE)
                tiles.append((j, r, lo, hi, hi == (r + 1) * TILE, lo == 0))

    def finish(g):
        return pltpu.make_async_copy(outs.at[g], out.at[:, wide(g)], sems.at[g])

    def head(g, carry):
        cols = pl.ds(pl.multiple_of(g * HD, HD), HD)
        vt[...] = v[:, cols].T
        fold(tiles, g, q, k.at[:, cols], vt, acc_out, stat_out)

        @pl.when(later[g] == 0)
        def _():
            write_out(g, acc_out, stat_out, outs)
            finish(g).start()

        return carry

    lax.fori_loop(0, KVH, head, 0)
    for g in range(KVH):
        pl.when(later[g] == 0)(finish(g).wait)
    for own in (False, True):
        cut_copies("wait", own, *args)


def near_kernel(local_at, work, first, meta, q, k, v, ok, ov, acc, stat, _, acc_out, stat_out, out, *rest):
    sent, (vt, outs, later, sems, cut_sems) = rest[:-5], rest[-5:]
    args = (first, meta, k, v, ok, ov, sent, cut_sems)
    for own in (False, True):
        cut_copies("start", own, *args)
    count_heads(meta, later, work)

    def finish(g):
        return pltpu.make_async_copy(outs.at[g], out.at[:, wide(g)], sems.at[g])

    def head(g, carry):
        local = meta[local_at + g] > 0

        @pl.when(jnp.logical_or(local, later[g] > 0))
        def _():
            acc_out[g] = acc[g]
            stat_out[g] = stat[g]

        @pl.when(local)
        def _():
            cols = pl.ds(pl.multiple_of(g * HD, HD), HD)
            vt[...] = ov[:, cols].T
            fold(ALL_TILES, g, q, ok.at[:, cols], vt, acc_out, stat_out)

            @pl.when(later[g] == 0)
            def _():
                write_out(g, acc_out, stat_out, outs)
                finish(g).start()

        return carry

    lax.fori_loop(0, KVH, head, 0)
    for g in range(KVH):
        pl.when(jnp.logical_and(meta[local_at + g] > 0, later[g] == 0))(finish(g).wait)
    for own in (False, True):
        cut_copies("wait", own, *args)


def wide(g):
    return pl.ds(pl.multiple_of(g * WIDE, WIDE), WIDE)


def part(g, j):
    return pl.ds(pl.multiple_of(g * WIDE + j * HD, HD), HD)


def count_heads(meta, counts, *spans):
    for g in range(KVH):
        counts[g] = 0

    def count(i, carry):
        g = meta[i]

        @pl.when(g >= 0)
        def _():
            counts[g] = counts[g] + 1

        return carry

    for span in spans:
        lax.fori_loop(*span, count, 0)


def write_out(g, acc, stat, outs):
    for j in range(GROUP):
        total = stat[g, GROUP + j : GROUP + j + 1, :]
        outs[g, :, j * HD : (j + 1) * HD] = (acc[g, j] / total).astype(jnp.bfloat16).T


def fold(tiles, g, q, k, vt, acc, stat):
    low = lax.broadcasted_iota(jnp.int32, (TILE, TILE), 1) >= lax.broadcasted_iota(jnp.int32, (TILE, TILE), 0)
    peaks, sums, scores, weights = {}, {}, {}, {}
    fresh = {t[:2] for t in tiles if t[5]}
    for j, r in {t[:2]: None for t in tiles if t[:2] not in fresh}:
        at = slice(r * TILE, (r + 1) * TILE)
        peaks[j, r], sums[j, r] = stat[g, j : j + 1, at], stat[g, GROUP + j : GROUP + j + 1, at]

    def score(j, r, lo, hi, diagonal, first):
        s = scores_of(k[lo:hi, :], q[r * TILE : (r + 1) * TILE, part(g, j)])
        if diagonal:
            last = jnp.where(low, s[hi - lo - TILE :], -1e30)
            s = jnp.concatenate([s[: hi - lo - TILE], last], axis=0) if hi - lo > TILE else last
        return s

    def weigh(s, j, r, lo, hi, diagonal, first):
        m = jnp.max(s, axis=0, keepdims=True)
        m = m if first else jnp.maximum(peaks[j, r], m)
        w = jnp.exp2((s - m) * SCALE)
        total = jnp.sum(w, axis=0, keepdims=True)
        alpha = None
        if not first:
            alpha = jnp.exp2((peaks[j, r] - m) * SCALE)
            total = total + sums[j, r] * alpha
        peaks[j, r], sums[j, r] = m, total
        return w, alpha

    def gather(pair, j, r, lo, hi, diagonal, first):
        w, alpha = pair
        at = slice(r * TILE, (r + 1) * TILE)
        new = total_of(vt[:, lo:hi], w)
        acc[g, j, :, at] = new if first else acc[g, j, :, at] * alpha + new

    count = len(tiles)
    for t in range(count + 3):
        if t < count:
            scores[t] = score(*tiles[t])
        if 0 <= t - 2 < count:
            weights[t - 2] = weigh(scores.pop(t - 2), *tiles[t - 2])
        if 0 <= t - 3:
            gather(weights.pop(t - 3), *tiles[t - 3])
    for (j, r), m in peaks.items():
        at = slice(r * TILE, (r + 1) * TILE)
        stat[g, j : j + 1, at] = m
        stat[g, GROUP + j : GROUP + j + 1, at] = sums[j, r]


def far_kernel(n_here, n_swap, here_at, here_later, swap_at, swap_later, meta, *refs):
    arrived, refs = refs[:n_here], refs[n_here:]
    swapped, refs = refs[:n_swap], refs[n_swap:]
    q, acc, stat, _, acc_out, stat_out, out, outs, kv, vt, seen, here, later, kv_sem, out_sem = refs
    pieces = n_here + (swapped[0].shape[0] // (2 * BLK) if n_swap else 0)

    def finish(g):
        return pltpu.make_async_copy(outs.at[g], out.at[:, wide(g)], out_sem.at[g])

    for i in range(pieces):
        g = meta[here_at + i] if i < n_here else meta[swap_at + i - n_here]
        block = arrived[i] if i < n_here else swapped[0].at[pl.ds((i - n_here) * 2 * BLK, 2 * BLK), :]
        pl.when(g >= 0)(pltpu.make_async_copy(block, kv.at[i], kv_sem.at[i]).start)

    count_heads(meta, here, (here_at, here_at + n_here), (swap_at, swap_at + pieces - n_here))
    count_heads(meta, later, here_later, swap_later)
    for g in range(KVH):
        seen[g] = 0

        @pl.when(jnp.logical_and(later[g] > 0, here[g] == 0))
        def _():
            acc_out[g] = acc[g]
            stat_out[g] = stat[g]

    def piece(i, carry):
        g = meta[jnp.where(i < n_here, here_at + i, swap_at + i - n_here)]

        @pl.when(g >= 0)
        def _():
            @pl.when(seen[g] == 0)
            def _():
                acc_out[g] = acc[g]
                stat_out[g] = stat[g]

            pltpu.make_async_copy(kv.at[i], kv.at[i], kv_sem.at[i]).wait()
            vt[...] = kv[i, BLK:, :].T
            fold(ALL_TILES, g, q, kv.at[i, pl.ds(0, BLK), :], vt, acc_out, stat_out)
            seen[g] = seen[g] + 1

            @pl.when(jnp.logical_and(seen[g] == here[g], later[g] == 0))
            def _():
                write_out(g, acc_out, stat_out, outs)
                finish(g).start()

        return carry

    lax.fori_loop(0, pieces, piece, 0)
    for g in range(KVH):
        pl.when(jnp.logical_and(here[g] > 0, later[g] == 0))(finish(g).wait)


def pack_kernel(count, *refs):
    joined = refs[count + 1]
    for i in range(count):
        joined[i * 2 * BLK : (i + 1) * 2 * BLK, :] = refs[i][...]
    refs[count + 2][...] = refs[count][...]


def body(queries, key, value, selection):
    me, side = lax.axis_index("ctx"), lax.axis_index("head")
    peers = lax.axis_size("ctx")
    order, table, groups = patterns(peers)
    total = len(order)
    swap = [(0, 1), (1, 0)]
    okey, ovalue = lax.ppermute(key, "head", swap), lax.ppermute(value, "head", swap)

    ends = lax.dynamic_index_in_dim(jnp.asarray(table), me, 0, keepdims=False)
    targets, sources = ends[:total], ends[total:]
    picks = selection[:, :, 1:]
    asked = lax.dynamic_slice_in_dim(picks, side * KVG, KVG, 1)
    codes = (asked - 2 * me) * KVH + (side * KVG + jnp.arange(KVG, dtype=jnp.int32))[None, :, None] + 1
    wanted = jnp.max(
        jnp.where((asked >> 1) == me, codes, 0).reshape(peers, 2 * KVG * TOPK), axis=1
    )
    cuts = jnp.max(
        jnp.where(targets[:, None] == jnp.arange(peers, dtype=jnp.int32)[None, :], wanted[None, :], 0), axis=1
    )
    mine = lax.dynamic_slice_in_dim(picks, 2 * me + side, 1, 0)[0]
    owners = jnp.where(mine >= 0, mine >> 1, -1)
    local = jnp.any(owners == me, axis=1).astype(jnp.int32)
    heads = jnp.arange(KVH, dtype=jnp.int32)
    hit = jnp.any(owners[None, :, :] == sources[:, None, None], axis=2)
    near = (heads // KVG) == side
    work_here = jnp.max(jnp.where(hit & near, heads, -1), axis=1)
    work_swap = jnp.max(jnp.where(hit & ~near, heads, -1), axis=1)
    meta = jnp.concatenate([side[None].astype(jnp.int32), cuts, local, work_here, work_swap])
    local_at = 1 + total
    here_at = local_at + KVH
    swap_at = here_at + total
    end = swap_at + total

    piece_shape = jax.ShapeDtypeStruct((2 * BLK, HD), jnp.bfloat16)
    any_spec, vmem_spec = pl.BlockSpec(memory_space=ANY), pl.BlockSpec(memory_space=VMEM)
    state = (
        jax.ShapeDtypeStruct((KVH, GROUP, HD, BLK), jnp.float32),
        jax.ShapeDtypeStruct((KVH, 2 * GROUP, BLK), jnp.float32),
        jax.ShapeDtypeStruct((BLK, QH * HD), jnp.bfloat16),
    )
    params = pltpu.CompilerParams(vmem_limit_bytes=16 << 20)

    firsts = [0, groups[0][1], groups[1][1], total]
    counts = [b - a for a, b in zip(firsts[:-1], firsts[1:])]
    sent = pl.pallas_call(
        cut_kernel,
        grid_spec=pltpu.PrefetchScalarGridSpec(
            num_scalar_prefetch=1,
            grid=(),
            in_specs=[vmem_spec] * 4,
            out_specs=[any_spec] * counts[0],
            scratch_shapes=[pltpu.SemaphoreType.DMA((counts[0], 2))],
        ),
        out_shape=[piece_shape] * counts[0],
        compiler_params=params,
        cost_estimate=pl.CostEstimate(flops=0, bytes_accessed=1 << 10, transcendentals=0),
        name="cut",
    )(meta, key, value, okey, ovalue)

    def inner(kernel, name, first, count, *through):
        return pl.pallas_call(
            functools.partial(kernel, local_at, (here_at, end), first),
            grid_spec=pltpu.PrefetchScalarGridSpec(
                num_scalar_prefetch=1,
                grid=(),
                in_specs=[vmem_spec] * 5 + [vmem_spec, vmem_spec, any_spec][: len(through)],
                out_specs=[vmem_spec, vmem_spec] + [any_spec] * (1 + count),
                scratch_shapes=[
                    VMEM((HD, BLK), jnp.bfloat16),
                    VMEM((KVH, BLK, WIDE), jnp.bfloat16),
                    pltpu.SMEM((KVH,), jnp.int32),
                    pltpu.SemaphoreType.DMA((KVH,)),
                    pltpu.SemaphoreType.DMA((count, 2)),
                ],
            ),
            out_shape=(*state, *[piece_shape] * count),
            input_output_aliases={6 + i: i for i in range(len(through))},
            compiler_params=params,
            cost_estimate=pl.CostEstimate(
                flops=0, bytes_accessed=1 << 10, transcendentals=0
            ),
            name=name,
        )(meta, queries, key, value, okey, ovalue, *through)

    acc, stat, out, *second = inner(own_kernel, "own", firsts[1], counts[1])
    acc, stat, out, *third = inner(near_kernel, "near", firsts[2], counts[2], acc, stat, out)
    sent = [*sent, *second, *third]

    landed = [None] * total
    swapped = []

    def send(n):
        a, b = groups[n]
        for j in range(a, b):
            landed[j] = lax.ppermute(sent[j], "ctx", order[j])

    def pack(n, stat):
        a, b = groups[n]
        count = b - a
        joined, stat = pl.pallas_call(
            functools.partial(pack_kernel, count),
            in_specs=[vmem_spec] * (count + 1),
            out_specs=[vmem_spec] * 2,
            out_shape=(jax.ShapeDtypeStruct((count * 2 * BLK, HD), jnp.bfloat16), state[1]),
            input_output_aliases={count: 1},
            compiler_params=params,
            cost_estimate=pl.CostEstimate(flops=0, bytes_accessed=1 << 10, transcendentals=0),
            name="pack",
        )(*landed[a:b], stat)
        swapped.append(lax.ppermute(joined, "head", swap))
        return stat

    def far(here, swaps, acc, stat, out):
        a, b = groups[here] if here is not None else (0, 0)
        a0, b0 = groups[swaps] if swaps is not None else (0, 0)
        here_end = max(b, b0)
        swap_end = b0 if swaps is not None else (groups[here - 1][1] if here else 0)
        n_here = b - a
        pieces = n_here + b0 - a0
        others = [swapped[swaps]] if swaps is not None else []
        base = 1 + n_here + len(others)
        return pl.pallas_call(
            functools.partial(
                far_kernel, n_here, len(others),
                here_at + a, (here_at + here_end, swap_at), swap_at + a0, (swap_at + swap_end, end),
            ),
            grid_spec=pltpu.PrefetchScalarGridSpec(
                num_scalar_prefetch=1,
                grid=(),
                in_specs=[any_spec] * (base - 1) + [vmem_spec] * 3 + [any_spec],
                out_specs=[vmem_spec, vmem_spec, any_spec],
                scratch_shapes=[
                    VMEM((KVH, BLK, WIDE), jnp.bfloat16),
                    VMEM((pieces, 2 * BLK, HD), jnp.bfloat16),
                    VMEM((HD, BLK), jnp.bfloat16),
                    pltpu.SMEM((KVH,), jnp.int32),
                    pltpu.SMEM((KVH,), jnp.int32),
                    pltpu.SMEM((KVH,), jnp.int32),
                    pltpu.SemaphoreType.DMA((pieces,)),
                    pltpu.SemaphoreType.DMA((KVH,)),
                ],
            ),
            out_shape=state,
            input_output_aliases={base + 1 + i: i for i in range(3)},
            compiler_params=params,
            cost_estimate=pl.CostEstimate(
                flops=32 * pieces * ROWS * BLK * HD, bytes_accessed=pieces << 21, transcendentals=pieces * ROWS * BLK
            ),
            name="far",
        )(meta, *landed[a:b], *others, queries, acc, stat, out)

    for n in range(len(groups)):
        send(n)
    last = len(groups) - 1
    for n in range(last):
        stat = pack(n, stat)
        acc, stat, out = far(n, n - 1 if n else None, acc, stat, out)
    acc, stat, out = far(None, last - 1, acc, stat, out)
    stat = pack(last, stat)
    acc, stat, out = far(last, None, acc, stat, out)
    acc, stat, out = far(None, last, acc, stat, out)
    return out


def solution(mesh):
    placed = (P(("ctx", "head"), None), P(("ctx", "head"), None), P(("ctx", "head"), None), P())
    return jax.shard_map(
        body, mesh=mesh, in_specs=placed, out_specs=P(("ctx", "head"), None), check_vma=False
    )
```

```python
import functools
import math

import jax
import jax.numpy as jnp
import numpy as np
from jax import lax
from jax.experimental import pallas as pl
from jax.experimental.pallas import tpu as pltpu
from jax.sharding import PartitionSpec as P

QH = 32
KVH = 8
HD = 128
BLK = 512
TOPK = 3
GROUP = QH // KVH
KVG = KVH // 2
WIDE = GROUP * HD
ROWS = GROUP * BLK
SCALE = math.log2(math.e) / math.sqrt(HD)
TILE = 128
SPAN = 256
ALL_TILES = [
    (j, r, lo, lo + SPAN, False, False) for lo in range(0, BLK, SPAN) for j in range(GROUP) for r in range(BLK // TILE)
]
VMEM = pltpu.VMEM
ANY = pl.ANY


def patterns(peers):
    fast = 4 if peers % 4 == 0 else 1
    slow = peers // fast

    def permute(moves, flip):
        pairs = [(a * fast + f, b * fast + (f ^ flip)) for a, b in moves for f in range(fast)]
        return [(a, b) for a, b in pairs if a < b]

    level = [(a, a) for a in range(slow)]
    if (fast, slow) == (4, 4):
        two, one, zero = [(0, 2), (1, 3)], [(0, 3), (1, 2)], [(0, 1), (2, 3)]
        order = [permute(two, 0), permute(one, 0), permute(level, 1)]
        order += [permute(two, 1), permute(one, 1), permute(zero, 0), permute(level, 2)]
        order += [permute(two, 2), permute(one, 2), permute(zero, 1), permute(level, 3)]
        order += [permute(two, 3), permute(zero, 2), permute(zero, 3)]
        order += [permute(one, 3)]
        edges = [0, 3, 7, 11, 14, 15]
    else:
        order = []
        for m in range(fast):
            order += [permute([(a, a + d) for a in range(slow - d)], m) for d in range(1, slow)]
        order += [permute(level, m) for m in range(1, fast)]
        edges = [round(i * len(order) / 5) for i in range(6)]
    table = np.full((peers, 2 * len(order)), -2, np.int32)
    for n, pairs in enumerate(order):
        for a, b in pairs:
            table[a, n] = b
            table[b, len(order) + n] = a
    return order, table, list(zip(edges[:-1], edges[1:]))


def scores_of(k, q):
    return lax.dot_general(k, q, (((1,), (1,)), ((), ())), preferred_element_type=jnp.float32)


def total_of(vt, weights):
    return jnp.dot(vt, weights.astype(jnp.bfloat16), preferred_element_type=jnp.float32)


def cut_copies(act, own, first, meta, key, value, okey, ovalue, outs, sems):
    for j, to in enumerate(outs):
        code = meta[1 + first + j] - 1
        block, head = code // KVH, code % KVH
        col = pl.ds(pl.multiple_of(jnp.maximum(head, 0) * HD, HD), HD)
        flag = jnp.logical_and(code >= 0, (block == meta[0]) if own else (block != meta[0]))
        for t, source in enumerate((key, value) if own else (okey, ovalue)):
            copy = pltpu.make_async_copy(source.at[:, col], to.at[pl.ds(t * BLK, BLK), :], sems.at[j, t])
            pl.when(flag)(copy.start if act == "start" else copy.wait)


def cut_kernel(first, count, meta, key, value, okey, ovalue, *rest):
    *through, sems = rest
    outs = through[len(through) - count :]
    args = (first, meta, key, value, okey, ovalue, outs, sems)
    if len(through) > count:
        through[1][...] = through[0][...]
    for act in ("start", "wait"):
        for own in (False, True):
            cut_copies(act, own, *args)


def own_kernel(local_at, work, first, meta, q, k, v, ok, ov, acc_out, stat_out, out, *rest):
    sent, (vt, outs, later, sems, cut_sems) = rest[:-5], rest[-5:]
    args = (first, meta, k, v, ok, ov, sent, cut_sems)
    for own in (False, True):
        cut_copies("start", own, *args)
    count_heads(meta, later, work)
    for g in range(KVH):
        later[g] = later[g] + meta[local_at + g]
    tiles = []
    for lo in range(0, BLK, SPAN):
        for j in range(GROUP):
            for r in range(lo // TILE, BLK // TILE):
                hi = min(lo + SPAN, (r + 1) * TILE)
                tiles.append((j, r, lo, hi, hi == (r + 1) * TILE, lo == 0))

    def finish(g):
        return pltpu.make_async_copy(outs.at[g], out.at[:, wide(g)], sems.at[g])

    def head(g, carry):
        cols = pl.ds(pl.multiple_of(g * HD, HD), HD)
        vt[...] = v[:, cols].T
        fold(tiles, g, q, k.at[:, cols], vt, acc_out, stat_out)

        @pl.when(later[g] == 0)
        def _():
            write_out(g, acc_out, stat_out, outs)
            finish(g).start()

        return carry

    lax.fori_loop(0, KVH, head, 0)
    for g in range(KVH):
        pl.when(later[g] == 0)(finish(g).wait)
    for own in (False, True):
        cut_copies("wait", own, *args)


def near_kernel(local_at, work, meta, q, ok, ov, acc, stat, _, acc_out, stat_out, out, vt, outs, later, sems):
    count_heads(meta, later, work)

    def finish(g):
        return pltpu.make_async_copy(outs.at[g], out.at[:, wide(g)], sems.at[g])

    def head(g, carry):
        local = meta[local_at + g] > 0

        @pl.when(jnp.logical_or(local, later[g] > 0))
        def _():
            acc_out[g] = acc[g]
            stat_out[g] = stat[g]

        @pl.when(local)
        def _():
            cols = pl.ds(pl.multiple_of(g * HD, HD), HD)
            vt[...] = ov[:, cols].T
            fold(ALL_TILES, g, q, ok.at[:, cols], vt, acc_out, stat_out)

            @pl.when(later[g] == 0)
            def _():
                write_out(g, acc_out, stat_out, outs)
                finish(g).start()

        return carry

    lax.fori_loop(0, KVH, head, 0)
    for g in range(KVH):
        pl.when(jnp.logical_and(meta[local_at + g] > 0, later[g] == 0))(finish(g).wait)


def wide(g):
    return pl.ds(pl.multiple_of(g * WIDE, WIDE), WIDE)


def part(g, j):
    return pl.ds(pl.multiple_of(g * WIDE + j * HD, HD), HD)


def count_heads(meta, counts, *spans):
    for g in range(KVH):
        counts[g] = 0

    def count(i, carry):
        g = meta[i]

        @pl.when(g >= 0)
        def _():
            counts[g] = counts[g] + 1

        return carry

    for span in spans:
        lax.fori_loop(*span, count, 0)


def write_out(g, acc, stat, outs):
    for j in range(GROUP):
        total = stat[g, GROUP + j : GROUP + j + 1, :]
        outs[g, :, j * HD : (j + 1) * HD] = (acc[g, j] / total).astype(jnp.bfloat16).T


def fold(tiles, g, q, k, vt, acc, stat):
    low = lax.broadcasted_iota(jnp.int32, (TILE, TILE), 1) >= lax.broadcasted_iota(jnp.int32, (TILE, TILE), 0)
    peaks, sums, scores, weights = {}, {}, {}, {}
    fresh = {t[:2] for t in tiles if t[5]}
    for j, r in {t[:2]: None for t in tiles if t[:2] not in fresh}:
        at = slice(r * TILE, (r + 1) * TILE)
        peaks[j, r], sums[j, r] = stat[g, j : j + 1, at], stat[g, GROUP + j : GROUP + j + 1, at]

    def score(j, r, lo, hi, diagonal, first):
        s = scores_of(k[lo:hi, :], q[r * TILE : (r + 1) * TILE, part(g, j)])
        if diagonal:
            last = jnp.where(low, s[hi - lo - TILE :], -1e30)
            s = jnp.concatenate([s[: hi - lo - TILE], last], axis=0) if hi - lo > TILE else last
        return s

    def weigh(s, j, r, lo, hi, diagonal, first):
        m = jnp.max(s, axis=0, keepdims=True)
        m = m if first else jnp.maximum(peaks[j, r], m)
        w = jnp.exp2((s - m) * SCALE)
        total = jnp.sum(w, axis=0, keepdims=True)
        alpha = None
        if not first:
            alpha = jnp.exp2((peaks[j, r] - m) * SCALE)
            total = total + sums[j, r] * alpha
        peaks[j, r], sums[j, r] = m, total
        return w, alpha

    def gather(pair, j, r, lo, hi, diagonal, first):
        w, alpha = pair
        at = slice(r * TILE, (r + 1) * TILE)
        new = total_of(vt[:, lo:hi], w)
        acc[g, j, :, at] = new if first else acc[g, j, :, at] * alpha + new

    count = len(tiles)
    for t in range(count + 3):
        if t < count:
            scores[t] = score(*tiles[t])
        if 0 <= t - 2 < count:
            weights[t - 2] = weigh(scores.pop(t - 2), *tiles[t - 2])
        if 0 <= t - 3:
            gather(weights.pop(t - 3), *tiles[t - 3])
    for (j, r), m in peaks.items():
        at = slice(r * TILE, (r + 1) * TILE)
        stat[g, j : j + 1, at] = m
        stat[g, GROUP + j : GROUP + j + 1, at] = sums[j, r]


def far_kernel(n_here, n_swap, local_at, here_at, here_later, swap_at, swap_later, meta, *refs):
    arrived, refs = refs[:n_here], refs[n_here:]
    swapped, refs = refs[:n_swap], refs[n_swap:]
    q, acc, stat, _, acc_out, stat_out, out, outs, kv, vt, seen, here, later, kv_sem, out_sem = refs
    pieces = n_here + (swapped[0].shape[0] // (2 * BLK) if n_swap else 0)

    def finish(g):
        return pltpu.make_async_copy(outs.at[g], out.at[:, wide(g)], out_sem.at[g])

    for i in range(pieces):
        g = meta[here_at + i] if i < n_here else meta[swap_at + i - n_here]
        block = arrived[i] if i < n_here else swapped[0].at[pl.ds((i - n_here) * 2 * BLK, 2 * BLK), :]
        pl.when(g >= 0)(pltpu.make_async_copy(block, kv.at[i], kv_sem.at[i]).start)

    count_heads(meta, here, (here_at, here_at + n_here), (swap_at, swap_at + pieces - n_here))
    count_heads(meta, later, here_later, swap_later)
    for g in range(KVH):
        seen[g] = 0
        if local_at is not None:
            later[g] = later[g] + meta[local_at + g]

        @pl.when(jnp.logical_and(later[g] > 0, here[g] == 0))
        def _():
            acc_out[g] = acc[g]
            stat_out[g] = stat[g]

    def piece(i, carry):
        g = meta[jnp.where(i < n_here, here_at + i, swap_at + i - n_here)]

        @pl.when(g >= 0)
        def _():
            @pl.when(seen[g] == 0)
            def _():
                acc_out[g] = acc[g]
                stat_out[g] = stat[g]

            pltpu.make_async_copy(kv.at[i], kv.at[i], kv_sem.at[i]).wait()
            vt[...] = kv[i, BLK:, :].T
            fold(ALL_TILES, g, q, kv.at[i, pl.ds(0, BLK), :], vt, acc_out, stat_out)
            seen[g] = seen[g] + 1

            @pl.when(jnp.logical_and(seen[g] == here[g], later[g] == 0))
            def _():
                write_out(g, acc_out, stat_out, outs)
                finish(g).start()

        return carry

    lax.fori_loop(0, pieces, piece, 0)
    for g in range(KVH):
        pl.when(jnp.logical_and(here[g] > 0, later[g] == 0))(finish(g).wait)


def pack_kernel(count, *refs):
    joined = refs[count + 1]
    for i in range(count):
        joined[i * 2 * BLK : (i + 1) * 2 * BLK, :] = refs[i][...]
    refs[count + 2][...] = refs[count][...]


def body(queries, key, value, selection):
    me, side = lax.axis_index("ctx"), lax.axis_index("head")
    peers = lax.axis_size("ctx")
    order, table, groups = patterns(peers)
    total = len(order)
    swap = [(0, 1), (1, 0)]
    okey, ovalue = lax.ppermute(key, "head", swap), lax.ppermute(value, "head", swap)

    ends = lax.dynamic_index_in_dim(jnp.asarray(table), me, 0, keepdims=False)
    targets, sources = ends[:total], ends[total:]
    picks = selection[:, :, 1:]
    asked = lax.dynamic_slice_in_dim(picks, side * KVG, KVG, 1)
    codes = (asked - 2 * me) * KVH + (side * KVG + jnp.arange(KVG, dtype=jnp.int32))[None, :, None] + 1
    wanted = jnp.max(
        jnp.where((asked >> 1) == me, codes, 0).reshape(peers, 2 * KVG * TOPK), axis=1
    )
    cuts = jnp.max(
        jnp.where(targets[:, None] == jnp.arange(peers, dtype=jnp.int32)[None, :], wanted[None, :], 0), axis=1
    )
    mine = lax.dynamic_slice_in_dim(picks, 2 * me + side, 1, 0)[0]
    owners = jnp.where(mine >= 0, mine >> 1, -1)
    local = jnp.any(owners == me, axis=1).astype(jnp.int32)
    heads = jnp.arange(KVH, dtype=jnp.int32)
    hit = jnp.any(owners[None, :, :] == sources[:, None, None], axis=2)
    near = (heads // KVG) == side
    work_here = jnp.max(jnp.where(hit & near, heads, -1), axis=1)
    work_swap = jnp.max(jnp.where(hit & ~near, heads, -1), axis=1)
    meta = jnp.concatenate([side[None].astype(jnp.int32), cuts, local, work_here, work_swap])
    local_at = 1 + total
    here_at = local_at + KVH
    swap_at = here_at + total
    end = swap_at + total

    piece_shape = jax.ShapeDtypeStruct((2 * BLK, HD), jnp.bfloat16)
    any_spec, vmem_spec = pl.BlockSpec(memory_space=ANY), pl.BlockSpec(memory_space=VMEM)
    state = (
        jax.ShapeDtypeStruct((KVH, GROUP, HD, BLK), jnp.float32),
        jax.ShapeDtypeStruct((KVH, 2 * GROUP, BLK), jnp.float32),
        jax.ShapeDtypeStruct((BLK, QH * HD), jnp.bfloat16),
    )
    params = pltpu.CompilerParams(vmem_limit_bytes=16 << 20)

    firsts, counts = [a for a, _ in groups], [b - a for a, b in groups]
    quick = pl.CostEstimate(flops=0, bytes_accessed=1 << 10, transcendentals=0)

    def cut(first, count, *through):
        return pl.pallas_call(
            functools.partial(cut_kernel, first, count),
            grid_spec=pltpu.PrefetchScalarGridSpec(
                num_scalar_prefetch=1,
                grid=(),
                in_specs=[vmem_spec] * (4 + len(through)),
                out_specs=[vmem_spec] * len(through) + [any_spec] * count,
                scratch_shapes=[pltpu.SemaphoreType.DMA((count, 2))],
            ),
            out_shape=[*[state[1]] * len(through), *[piece_shape] * count],
            input_output_aliases={5 + i: i for i in range(len(through))},
            compiler_params=params,
            cost_estimate=quick,
            name="cut",
        )(meta, key, value, okey, ovalue, *through)

    work_scratch = [
        VMEM((HD, BLK), jnp.bfloat16),
        VMEM((KVH, BLK, WIDE), jnp.bfloat16),
        pltpu.SMEM((KVH,), jnp.int32),
        pltpu.SemaphoreType.DMA((KVH,)),
    ]
    first = cut(0, firsts[1])
    acc, stat, out, *second = pl.pallas_call(
        functools.partial(own_kernel, local_at, (here_at, end), firsts[1]),
        grid_spec=pltpu.PrefetchScalarGridSpec(
            num_scalar_prefetch=1,
            grid=(),
            in_specs=[vmem_spec] * 5,
            out_specs=[vmem_spec, vmem_spec] + [any_spec] * (1 + counts[1]),
            scratch_shapes=work_scratch + [pltpu.SemaphoreType.DMA((counts[1], 2))],
        ),
        out_shape=(*state, *[piece_shape] * counts[1]),
        compiler_params=params,
        cost_estimate=quick,
        name="own",
    )(meta, queries, key, value, okey, ovalue)
    sent = [*first, *second]

    def near(start, acc, stat, out):
        return pl.pallas_call(
            functools.partial(near_kernel, local_at, (start, end)),
            grid_spec=pltpu.PrefetchScalarGridSpec(
                num_scalar_prefetch=1,
                grid=(),
                in_specs=[vmem_spec] * 5 + [any_spec],
                out_specs=[vmem_spec, vmem_spec, any_spec],
                scratch_shapes=work_scratch,
            ),
            out_shape=state,
            input_output_aliases={4 + i: i for i in range(3)},
            compiler_params=params,
            cost_estimate=pl.CostEstimate(
                flops=64 * ROWS * BLK * HD, bytes_accessed=4 << 20, transcendentals=8 * ROWS * BLK
            ),
            name="near",
        )(meta, queries, okey, ovalue, acc, stat, out)

    landed = [None] * total
    swapped = []

    def send(n):
        a, b = groups[n]
        for j in range(a, b):
            landed[j] = lax.ppermute(sent[j], "ctx", order[j])

    def pack(n, stat):
        a, b = groups[n]
        count = b - a
        joined, stat = pl.pallas_call(
            functools.partial(pack_kernel, count),
            in_specs=[vmem_spec] * (count + 1),
            out_specs=[vmem_spec] * 2,
            out_shape=(jax.ShapeDtypeStruct((count * 2 * BLK, HD), jnp.bfloat16), state[1]),
            input_output_aliases={count: 1},
            compiler_params=params,
            cost_estimate=pl.CostEstimate(flops=0, bytes_accessed=1 << 10, transcendentals=0),
            name="pack",
        )(*landed[a:b], stat)
        swapped.append(lax.ppermute(joined, "head", swap))
        return stat

    def far(here, swaps, acc, stat, out, local=None):
        a, b = groups[here] if here is not None else (0, 0)
        a0, b0 = groups[swaps] if swaps is not None else (0, 0)
        here_end = max(b, b0)
        swap_end = b0 if swaps is not None else a
        n_here = b - a
        pieces = n_here + b0 - a0
        others = [swapped[swaps]] if swaps is not None else []
        base = 1 + n_here + len(others)
        return pl.pallas_call(
            functools.partial(
                far_kernel, n_here, len(others), local,
                here_at + a, (here_at + here_end, swap_at), swap_at + a0, (swap_at + swap_end, end),
            ),
            grid_spec=pltpu.PrefetchScalarGridSpec(
                num_scalar_prefetch=1,
                grid=(),
                in_specs=[any_spec] * (base - 1) + [vmem_spec] * 3 + [any_spec],
                out_specs=[vmem_spec, vmem_spec, any_spec],
                scratch_shapes=[
                    VMEM((KVH, BLK, WIDE), jnp.bfloat16),
                    VMEM((pieces, 2 * BLK, HD), jnp.bfloat16),
                    VMEM((HD, BLK), jnp.bfloat16),
                    pltpu.SMEM((KVH,), jnp.int32),
                    pltpu.SMEM((KVH,), jnp.int32),
                    pltpu.SMEM((KVH,), jnp.int32),
                    pltpu.SemaphoreType.DMA((pieces,)),
                    pltpu.SemaphoreType.DMA((KVH,)),
                ],
            ),
            out_shape=state,
            input_output_aliases={base + 1 + i: i for i in range(3)},
            compiler_params=params,
            cost_estimate=pl.CostEstimate(
                flops=32 * pieces * ROWS * BLK * HD, bytes_accessed=pieces << 21, transcendentals=pieces * ROWS * BLK
            ),
            name="far",
        )(meta, *landed[a:b], *others, queries, acc, stat, out)

    send(0)
    send(1)
    for n in range(len(groups)):
        if n + 2 < len(groups):
            a, b = groups[n + 2]
            stat, *more = cut(a, b - a, stat)
            sent += more
            send(n + 2)
        stat = pack(n, stat)
        acc, stat, out = far(n, None, acc, stat, out, None if n else local_at)
        if n == 0:
            acc, stat, out = near(here_at + groups[0][1], acc, stat, out)
        acc, stat, out = far(None, n, acc, stat, out)
    return out


def solution(mesh):
    placed = (P(("ctx", "head"), None), P(("ctx", "head"), None), P(("ctx", "head"), None), P())
    return jax.shard_map(
        body, mesh=mesh, in_specs=placed, out_specs=P(("ctx", "head"), None), check_vma=False
    )
```

```python
import functools
import math

import jax
import jax.numpy as jnp
import numpy as np
from jax import lax
from jax.experimental import pallas as pl
from jax.experimental.pallas import tpu as pltpu
from jax.sharding import PartitionSpec as P

QH = 32
KVH = 8
HD = 128
BLK = 512
TOPK = 3
GROUP = QH // KVH
KVG = KVH // 2
WIDE = GROUP * HD
ROWS = GROUP * BLK
SCALE = math.log2(math.e) / math.sqrt(HD)
TILE = 128
SPAN = 256
ALL_TILES = [
    (j, r, lo, lo + SPAN, False, False) for lo in range(0, BLK, SPAN) for j in range(GROUP) for r in range(BLK // TILE)
]
VMEM = pltpu.VMEM
ANY = pl.ANY


def patterns(peers):
    fast = 4 if peers % 4 == 0 else 1
    slow = peers // fast

    def permute(moves, flip):
        pairs = [(a * fast + f, b * fast + (f ^ flip)) for a, b in moves for f in range(fast)]
        return [(a, b) for a, b in pairs if a < b]

    level = [(a, a) for a in range(slow)]
    if (fast, slow) == (4, 4):
        two, one, zero = [(0, 2), (1, 3)], [(0, 3), (1, 2)], [(0, 1), (2, 3)]
        order = [permute(two, 0), permute(level, 1), permute(level, 2), permute(level, 3)]
        order += [permute(one, 0), permute(two, 1), permute(one, 1)]
        order += [permute(two, 2), permute(one, 2), permute(zero, 0), permute(zero, 1)]
        order += [permute(two, 3), permute(zero, 2), permute(zero, 3)]
        order += [permute(one, 3)]
        edges = [0, 4, 7, 11, 14, 15]
    else:
        order = []
        for m in range(fast):
            order += [permute([(a, a + d) for a in range(slow - d)], m) for d in range(1, slow)]
        order += [permute(level, m) for m in range(1, fast)]
        edges = [round(i * len(order) / 5) for i in range(6)]
    table = np.full((peers, 2 * len(order)), -2, np.int32)
    for n, pairs in enumerate(order):
        for a, b in pairs:
            table[a, n] = b
            table[b, len(order) + n] = a
    return order, table, list(zip(edges[:-1], edges[1:]))


def scores_of(k, q):
    return lax.dot_general(k, q, (((1,), (1,)), ((), ())), preferred_element_type=jnp.float32)


def total_of(vt, weights):
    return jnp.dot(vt, weights.astype(jnp.bfloat16), preferred_element_type=jnp.float32)


def cut_copies(act, own, first, meta, key, value, okey, ovalue, outs, sems):
    for j, to in enumerate(outs):
        code = meta[1 + first + j] - 1
        block, head = code // KVH, code % KVH
        col = pl.ds(pl.multiple_of(jnp.maximum(head, 0) * HD, HD), HD)
        flag = jnp.logical_and(code >= 0, (block == meta[0]) if own else (block != meta[0]))
        for t, source in enumerate((key, value) if own else (okey, ovalue)):
            copy = pltpu.make_async_copy(source.at[:, col], to.at[pl.ds(t * BLK, BLK), :], sems.at[j, t])
            pl.when(flag)(copy.start if act == "start" else copy.wait)


def cut_kernel(first, count, meta, key, value, okey, ovalue, *rest):
    *through, sems = rest
    outs = through[len(through) - count :]
    args = (first, meta, key, value, okey, ovalue, outs, sems)
    if len(through) > count:
        through[1][...] = through[0][...]
    for act in ("start", "wait"):
        for own in (False, True):
            cut_copies(act, own, *args)


def own_kernel(local_at, work, first, meta, q, k, v, ok, ov, acc_out, stat_out, out, *rest):
    sent, (vt, outs, later, sems, cut_sems) = rest[:-5], rest[-5:]
    args = (first, meta, k, v, ok, ov, sent, cut_sems)
    for own in (False, True):
        cut_copies("start", own, *args)
    count_heads(meta, later, work)
    for g in range(KVH):
        later[g] = later[g] + meta[local_at + g]
    tiles = []
    for lo in range(0, BLK, SPAN):
        for j in range(GROUP):
            for r in range(lo // TILE, BLK // TILE):
                hi = min(lo + SPAN, (r + 1) * TILE)
                tiles.append((j, r, lo, hi, hi == (r + 1) * TILE, lo == 0))

    def finish(g):
        return pltpu.make_async_copy(outs.at[g], out.at[:, wide(g)], sems.at[g])

    def head(g, carry):
        cols = pl.ds(pl.multiple_of(g * HD, HD), HD)
        vt[...] = v[:, cols].T
        fold(tiles, g, q, k.at[:, cols], vt, acc_out, stat_out)

        @pl.when(later[g] == 0)
        def _():
            write_out(g, acc_out, stat_out, outs)
            finish(g).start()

        return carry

    lax.fori_loop(0, KVH, head, 0)
    for g in range(KVH):
        pl.when(later[g] == 0)(finish(g).wait)
    for own in (False, True):
        cut_copies("wait", own, *args)


def near_kernel(local_at, work, first, meta, q, k, v, ok, ov, acc, stat, _, acc_out, stat_out, out, *rest):
    sent, (vt, outs, later, sems, cut_sems) = rest[:-5], rest[-5:]
    args = (first, meta, k, v, ok, ov, sent, cut_sems)
    for own in (False, True):
        cut_copies("start", own, *args)
    count_heads(meta, later, work)

    def finish(g):
        return pltpu.make_async_copy(outs.at[g], out.at[:, wide(g)], sems.at[g])

    def head(g, carry):
        local = meta[local_at + g] > 0

        @pl.when(jnp.logical_or(local, later[g] > 0))
        def _():
            acc_out[g] = acc[g]
            stat_out[g] = stat[g]

        @pl.when(local)
        def _():
            cols = pl.ds(pl.multiple_of(g * HD, HD), HD)
            vt[...] = ov[:, cols].T
            fold(ALL_TILES, g, q, ok.at[:, cols], vt, acc_out, stat_out)

            @pl.when(later[g] == 0)
            def _():
                write_out(g, acc_out, stat_out, outs)
                finish(g).start()

        return carry

    lax.fori_loop(0, KVH, head, 0)
    for g in range(KVH):
        pl.when(jnp.logical_and(meta[local_at + g] > 0, later[g] == 0))(finish(g).wait)
    for own in (False, True):
        cut_copies("wait", own, *args)


def wide(g):
    return pl.ds(pl.multiple_of(g * WIDE, WIDE), WIDE)


def part(g, j):
    return pl.ds(pl.multiple_of(g * WIDE + j * HD, HD), HD)


def count_heads(meta, counts, *spans):
    for g in range(KVH):
        counts[g] = 0

    def count(i, carry):
        g = meta[i]

        @pl.when(g >= 0)
        def _():
            counts[g] = counts[g] + 1

        return carry

    for span in spans:
        lax.fori_loop(*span, count, 0)


def write_out(g, acc, stat, outs):
    for j in range(GROUP):
        total = stat[g, GROUP + j : GROUP + j + 1, :]
        outs[g, :, j * HD : (j + 1) * HD] = (acc[g, j] / total).astype(jnp.bfloat16).T


def fold(tiles, g, q, k, vt, acc, stat):
    low = lax.broadcasted_iota(jnp.int32, (TILE, TILE), 1) >= lax.broadcasted_iota(jnp.int32, (TILE, TILE), 0)
    peaks, sums, scores, weights = {}, {}, {}, {}
    fresh = {t[:2] for t in tiles if t[5]}
    for j, r in {t[:2]: None for t in tiles if t[:2] not in fresh}:
        at = slice(r * TILE, (r + 1) * TILE)
        peaks[j, r], sums[j, r] = stat[g, j : j + 1, at], stat[g, GROUP + j : GROUP + j + 1, at]

    def score(j, r, lo, hi, diagonal, first):
        s = scores_of(k[lo:hi, :], q[r * TILE : (r + 1) * TILE, part(g, j)])
        if diagonal:
            last = jnp.where(low, s[hi - lo - TILE :], -1e30)
            s = jnp.concatenate([s[: hi - lo - TILE], last], axis=0) if hi - lo > TILE else last
        return s

    def weigh(s, j, r, lo, hi, diagonal, first):
        m = jnp.max(s, axis=0, keepdims=True)
        m = m if first else jnp.maximum(peaks[j, r], m)
        w = jnp.exp2((s - m) * SCALE)
        total = jnp.sum(w, axis=0, keepdims=True)
        alpha = None
        if not first:
            alpha = jnp.exp2((peaks[j, r] - m) * SCALE)
            total = total + sums[j, r] * alpha
        peaks[j, r], sums[j, r] = m, total
        return w, alpha

    def gather(pair, j, r, lo, hi, diagonal, first):
        w, alpha = pair
        at = slice(r * TILE, (r + 1) * TILE)
        new = total_of(vt[:, lo:hi], w)
        acc[g, j, :, at] = new if first else acc[g, j, :, at] * alpha + new

    count = len(tiles)
    for t in range(count + 3):
        if t < count:
            scores[t] = score(*tiles[t])
        if 0 <= t - 2 < count:
            weights[t - 2] = weigh(scores.pop(t - 2), *tiles[t - 2])
        if 0 <= t - 3:
            gather(weights.pop(t - 3), *tiles[t - 3])
    for (j, r), m in peaks.items():
        at = slice(r * TILE, (r + 1) * TILE)
        stat[g, j : j + 1, at] = m
        stat[g, GROUP + j : GROUP + j + 1, at] = sums[j, r]


def far_kernel(n_here, n_swap, here_at, here_later, swap_at, swap_later, meta, *refs):
    arrived, refs = refs[:n_here], refs[n_here:]
    swapped, refs = refs[:n_swap], refs[n_swap:]
    q, acc, stat, _, acc_out, stat_out, out, outs, kv, vt, seen, here, later, kv_sem, out_sem = refs
    pieces = n_here + (swapped[0].shape[0] // (2 * BLK) if n_swap else 0)

    def finish(g):
        return pltpu.make_async_copy(outs.at[g], out.at[:, wide(g)], out_sem.at[g])

    for i in range(pieces):
        g = meta[here_at + i] if i < n_here else meta[swap_at + i - n_here]
        block = arrived[i] if i < n_here else swapped[0].at[pl.ds((i - n_here) * 2 * BLK, 2 * BLK), :]
        pl.when(g >= 0)(pltpu.make_async_copy(block, kv.at[i], kv_sem.at[i]).start)

    count_heads(meta, here, (here_at, here_at + n_here), (swap_at, swap_at + pieces - n_here))
    count_heads(meta, later, here_later, swap_later)
    for g in range(KVH):
        seen[g] = 0

        @pl.when(jnp.logical_and(later[g] > 0, here[g] == 0))
        def _():
            acc_out[g] = acc[g]
            stat_out[g] = stat[g]

    def piece(i, carry):
        g = meta[jnp.where(i < n_here, here_at + i, swap_at + i - n_here)]

        @pl.when(g >= 0)
        def _():
            @pl.when(seen[g] == 0)
            def _():
                acc_out[g] = acc[g]
                stat_out[g] = stat[g]

            pltpu.make_async_copy(kv.at[i], kv.at[i], kv_sem.at[i]).wait()
            vt[...] = kv[i, BLK:, :].T
            fold(ALL_TILES, g, q, kv.at[i, pl.ds(0, BLK), :], vt, acc_out, stat_out)
            seen[g] = seen[g] + 1

            @pl.when(jnp.logical_and(seen[g] == here[g], later[g] == 0))
            def _():
                write_out(g, acc_out, stat_out, outs)
                finish(g).start()

        return carry

    lax.fori_loop(0, pieces, piece, 0)
    for g in range(KVH):
        pl.when(jnp.logical_and(here[g] > 0, later[g] == 0))(finish(g).wait)


def pack_kernel(count, *refs):
    joined = refs[count + 1]
    for i in range(count):
        joined[i * 2 * BLK : (i + 1) * 2 * BLK, :] = refs[i][...]
    refs[count + 2][...] = refs[count][...]


def body(queries, key, value, selection):
    me, side = lax.axis_index("ctx"), lax.axis_index("head")
    peers = lax.axis_size("ctx")
    order, table, groups = patterns(peers)
    total = len(order)
    swap = [(0, 1), (1, 0)]
    okey, ovalue = lax.ppermute(key, "head", swap), lax.ppermute(value, "head", swap)

    ends = lax.dynamic_index_in_dim(jnp.asarray(table), me, 0, keepdims=False)
    targets, sources = ends[:total], ends[total:]
    picks = selection[:, :, 1:]
    asked = lax.dynamic_slice_in_dim(picks, side * KVG, KVG, 1)
    codes = (asked - 2 * me) * KVH + (side * KVG + jnp.arange(KVG, dtype=jnp.int32))[None, :, None] + 1
    wanted = jnp.max(
        jnp.where((asked >> 1) == me, codes, 0).reshape(peers, 2 * KVG * TOPK), axis=1
    )
    cuts = jnp.max(
        jnp.where(targets[:, None] == jnp.arange(peers, dtype=jnp.int32)[None, :], wanted[None, :], 0), axis=1
    )
    mine = lax.dynamic_slice_in_dim(picks, 2 * me + side, 1, 0)[0]
    owners = jnp.where(mine >= 0, mine >> 1, -1)
    local = jnp.any(owners == me, axis=1).astype(jnp.int32)
    heads = jnp.arange(KVH, dtype=jnp.int32)
    hit = jnp.any(owners[None, :, :] == sources[:, None, None], axis=2)
    near = (heads // KVG) == side
    work_here = jnp.max(jnp.where(hit & near, heads, -1), axis=1)
    work_swap = jnp.max(jnp.where(hit & ~near, heads, -1), axis=1)
    meta = jnp.concatenate([side[None].astype(jnp.int32), cuts, local, work_here, work_swap])
    local_at = 1 + total
    here_at = local_at + KVH
    swap_at = here_at + total
    end = swap_at + total

    piece_shape = jax.ShapeDtypeStruct((2 * BLK, HD), jnp.bfloat16)
    any_spec, vmem_spec = pl.BlockSpec(memory_space=ANY), pl.BlockSpec(memory_space=VMEM)
    state = (
        jax.ShapeDtypeStruct((KVH, GROUP, HD, BLK), jnp.float32),
        jax.ShapeDtypeStruct((KVH, 2 * GROUP, BLK), jnp.float32),
        jax.ShapeDtypeStruct((BLK, QH * HD), jnp.bfloat16),
    )
    params = pltpu.CompilerParams(vmem_limit_bytes=16 << 20)

    firsts = [0, groups[1][1], groups[2][1], groups[3][1]]
    counts = [b - a for a, b in zip(firsts[:-1], firsts[1:])]
    def cut(first, count, *through):
        return pl.pallas_call(
            functools.partial(cut_kernel, first, count),
            grid_spec=pltpu.PrefetchScalarGridSpec(
                num_scalar_prefetch=1,
                grid=(),
                in_specs=[vmem_spec] * (4 + len(through)),
                out_specs=[vmem_spec] * len(through) + [any_spec] * count,
                scratch_shapes=[pltpu.SemaphoreType.DMA((count, 2))],
            ),
            out_shape=[*[state[1]] * len(through), *[piece_shape] * count],
            input_output_aliases={5 + i: i for i in range(len(through))},
            compiler_params=params,
            cost_estimate=pl.CostEstimate(flops=0, bytes_accessed=1 << 10, transcendentals=0),
            name="cut",
        )(meta, key, value, okey, ovalue, *through)

    sent = cut(0, counts[0])

    def inner(kernel, name, first, count, *through):
        return pl.pallas_call(
            functools.partial(kernel, local_at, (here_at, end), first),
            grid_spec=pltpu.PrefetchScalarGridSpec(
                num_scalar_prefetch=1,
                grid=(),
                in_specs=[vmem_spec] * 5 + [vmem_spec, vmem_spec, any_spec][: len(through)],
                out_specs=[vmem_spec, vmem_spec] + [any_spec] * (1 + count),
                scratch_shapes=[
                    VMEM((HD, BLK), jnp.bfloat16),
                    VMEM((KVH, BLK, WIDE), jnp.bfloat16),
                    pltpu.SMEM((KVH,), jnp.int32),
                    pltpu.SemaphoreType.DMA((KVH,)),
                    pltpu.SemaphoreType.DMA((count, 2)),
                ],
            ),
            out_shape=(*state, *[piece_shape] * count),
            input_output_aliases={6 + i: i for i in range(len(through))},
            compiler_params=params,
            cost_estimate=pl.CostEstimate(
                flops=0, bytes_accessed=1 << 10, transcendentals=0
            ),
            name=name,
        )(meta, queries, key, value, okey, ovalue, *through)

    acc, stat, out, *second = inner(own_kernel, "own", firsts[1], counts[1])
    sent = [*sent, *second]

    landed = [None] * total
    swapped = []

    def send(n):
        a, b = groups[n]
        for j in range(a, b):
            landed[j] = lax.ppermute(sent[j], "ctx", order[j])

    def pack(n, stat):
        a, b = groups[n]
        count = b - a
        joined, stat = pl.pallas_call(
            functools.partial(pack_kernel, count),
            in_specs=[vmem_spec] * (count + 1),
            out_specs=[vmem_spec] * 2,
            out_shape=(jax.ShapeDtypeStruct((count * 2 * BLK, HD), jnp.bfloat16), state[1]),
            input_output_aliases={count: 1},
            compiler_params=params,
            cost_estimate=pl.CostEstimate(flops=0, bytes_accessed=1 << 10, transcendentals=0),
            name="pack",
        )(*landed[a:b], stat)
        swapped.append(lax.ppermute(joined, "head", swap))
        return stat

    def far(here, swaps, acc, stat, out):
        a, b = groups[here] if here is not None else (0, 0)
        a0, b0 = groups[swaps] if swaps is not None else (0, 0)
        here_end = max(b, b0)
        swap_end = b0 if swaps is not None else (groups[here - 1][1] if here else 0)
        n_here = b - a
        pieces = n_here + b0 - a0
        others = [swapped[swaps]] if swaps is not None else []
        base = 1 + n_here + len(others)
        return pl.pallas_call(
            functools.partial(
                far_kernel, n_here, len(others),
                here_at + a, (here_at + here_end, swap_at), swap_at + a0, (swap_at + swap_end, end),
            ),
            grid_spec=pltpu.PrefetchScalarGridSpec(
                num_scalar_prefetch=1,
                grid=(),
                in_specs=[any_spec] * (base - 1) + [vmem_spec] * 3 + [any_spec],
                out_specs=[vmem_spec, vmem_spec, any_spec],
                scratch_shapes=[
                    VMEM((KVH, BLK, WIDE), jnp.bfloat16),
                    VMEM((pieces, 2 * BLK, HD), jnp.bfloat16),
                    VMEM((HD, BLK), jnp.bfloat16),
                    pltpu.SMEM((KVH,), jnp.int32),
                    pltpu.SMEM((KVH,), jnp.int32),
                    pltpu.SMEM((KVH,), jnp.int32),
                    pltpu.SemaphoreType.DMA((pieces,)),
                    pltpu.SemaphoreType.DMA((KVH,)),
                ],
            ),
            out_shape=state,
            input_output_aliases={base + 1 + i: i for i in range(3)},
            compiler_params=params,
            cost_estimate=pl.CostEstimate(
                flops=32 * pieces * ROWS * BLK * HD, bytes_accessed=pieces << 21, transcendentals=pieces * ROWS * BLK
            ),
            name="far",
        )(meta, *landed[a:b], *others, queries, acc, stat, out)

    for n in range(3):
        send(n)
    stat = pack(0, stat)
    acc, stat, out, *third = inner(near_kernel, "near", firsts[2], counts[2], acc, stat, out)
    sent += third
    send(3)
    last = len(groups) - 1
    acc, stat, out = far(0, None, acc, stat, out)
    for n in range(1, last):
        stat = pack(n, stat)
        if n == last - 2:
            a, b = groups[last]
            stat, *final = cut(a, b - a, stat)
            sent += final
            send(last)
        acc, stat, out = far(n, n - 1, acc, stat, out)
    acc, stat, out = far(None, last - 1, acc, stat, out)
    stat = pack(last, stat)
    acc, stat, out = far(last, None, acc, stat, out)
    acc, stat, out = far(None, last, acc, stat, out)
    return out


def solution(mesh):
    placed = (P(("ctx", "head"), None), P(("ctx", "head"), None), P(("ctx", "head"), None), P())
    return jax.shard_map(
        body, mesh=mesh, in_specs=placed, out_specs=P(("ctx", "head"), None), check_vma=False
    )
```

```python
import functools
import math

import jax
import jax.numpy as jnp
import numpy as np
from jax import lax
from jax.experimental import pallas as pl
from jax.experimental.pallas import tpu as pltpu
from jax.sharding import PartitionSpec as P

QH = 32
KVH = 8
HD = 128
BLK = 512
TOPK = 3
GROUP = QH // KVH
KVG = KVH // 2
WIDE = GROUP * HD
ROWS = GROUP * BLK
SCALE = math.log2(math.e) / math.sqrt(HD)
TILE = 128
SPAN = 256
ALL_TILES = [
    (j, r, lo, lo + SPAN, False, False) for lo in range(0, BLK, SPAN) for j in range(GROUP) for r in range(BLK // TILE)
]
VMEM = pltpu.VMEM
ANY = pl.ANY


PAIR_TILES = [t for t in ALL_TILES if t[0] < 2]


def patterns(peers):
    fast = 4 if peers % 4 == 0 else 1
    slow = peers // fast

    def permute(moves, flip):
        pairs = [(a * fast + f, b * fast + (f ^ flip)) for a, b in moves for f in range(fast)]
        return [(a, b) for a, b in pairs if a < b]

    level = [(a, a) for a in range(slow)]
    if (fast, slow) == (4, 4):
        two, one, zero = [(0, 2), (1, 3)], [(0, 3), (1, 2)], [(0, 1), (2, 3)]
        order = [permute(two, 0), permute(level, 1), permute(level, 2), permute(level, 3)]
        order += [permute(one, 0), permute(two, 1), permute(one, 1)]
        order += [permute(two, 2), permute(one, 2), permute(zero, 0), permute(zero, 1)]
        order += [permute(two, 3), permute(zero, 2)]
        order += [permute(zero, 3), permute(one, 3)]
        edges = [0, 4, 7, 11, 13, 15]
    else:
        order = []
        for m in range(fast):
            order += [permute([(a, a + d) for a in range(slow - d)], m) for d in range(1, slow)]
        order += [permute(level, m) for m in range(1, fast)]
        edges = [round(i * len(order) / 5) for i in range(6)]
    table = np.full((peers, 2 * len(order)), -2, np.int32)
    for n, pairs in enumerate(order):
        for a, b in pairs:
            table[a, n] = b
            table[b, len(order) + n] = a
    return order, table, list(zip(edges[:-1], edges[1:]))


def scores_of(k, q):
    return lax.dot_general(k, q, (((1,), (1,)), ((), ())), preferred_element_type=jnp.float32)


def total_of(vt, weights):
    return jnp.dot(vt, weights.astype(jnp.bfloat16), preferred_element_type=jnp.float32)


def cut_copies(act, own, first, meta, key, value, okey, ovalue, outs, sems):
    for j, to in enumerate(outs):
        code = meta[1 + first + j] - 1
        block, head = code // KVH, code % KVH
        col = pl.ds(pl.multiple_of(jnp.maximum(head, 0) * HD, HD), HD)
        flag = jnp.logical_and(code >= 0, (block == meta[0]) if own else (block != meta[0]))
        for t, source in enumerate((key, value) if own else (okey, ovalue)):
            copy = pltpu.make_async_copy(source.at[:, col], to.at[pl.ds(t * BLK, BLK), :], sems.at[j, t])
            pl.when(flag)(copy.start if act == "start" else copy.wait)


def cut_kernel(first, count, meta, key, value, okey, ovalue, *rest):
    *through, sems = rest
    outs = through[len(through) - count :]
    args = (first, meta, key, value, okey, ovalue, outs, sems)
    if len(through) > count:
        through[1][...] = through[0][...]
    for act in ("start", "wait"):
        for own in (False, True):
            cut_copies(act, own, *args)


def own_kernel(local_at, work, first, meta, q, k, v, ok, ov, acc_out, stat_out, out, *rest):
    sent, (vt, outs, later, sems, cut_sems) = rest[:-5], rest[-5:]
    args = (first, meta, k, v, ok, ov, sent, cut_sems)
    for own in (False, True):
        cut_copies("start", own, *args)
    count_heads(meta, later, work)
    for g in range(KVH):
        later[g] = later[g] + meta[local_at + g]
    tiles = []
    for lo in range(0, BLK, SPAN):
        for j in range(2):
            for r in range(lo // TILE, BLK // TILE):
                hi = min(lo + SPAN, (r + 1) * TILE)
                tiles.append((j, r, lo, hi, hi == (r + 1) * TILE, lo == 0))

    def finish(g):
        return pltpu.make_async_copy(outs.at[g], out.at[:, wide(g)], sems.at[g])

    def head(g, carry):
        cols = pl.ds(pl.multiple_of(g * HD, HD), HD)
        vt[...] = v[:, cols].T

        def pair(h, carry):
            fold(tiles, g, q, k.at[:, cols], vt, acc_out, stat_out, 2 * h)
            return carry

        lax.fori_loop(0, GROUP // 2, pair, 0)

        @pl.when(later[g] == 0)
        def _():
            write_out(g, acc_out, stat_out, outs)
            finish(g).start()

        return carry

    lax.fori_loop(0, KVH, head, 0)
    for g in range(KVH):
        pl.when(later[g] == 0)(finish(g).wait)
    for own in (False, True):
        cut_copies("wait", own, *args)


def near_kernel(local_at, work, first, meta, q, k, v, ok, ov, acc, stat, _, acc_out, stat_out, out, *rest):
    sent, (vt, outs, later, sems, cut_sems) = rest[:-5], rest[-5:]
    args = (first, meta, k, v, ok, ov, sent, cut_sems)
    for own in (False, True):
        cut_copies("start", own, *args)
    count_heads(meta, later, work)

    def finish(g):
        return pltpu.make_async_copy(outs.at[g], out.at[:, wide(g)], sems.at[g])

    def head(g, carry):
        local = meta[local_at + g] > 0

        @pl.when(jnp.logical_or(local, later[g] > 0))
        def _():
            acc_out[g] = acc[g]
            stat_out[g] = stat[g]

        @pl.when(local)
        def _():
            cols = pl.ds(pl.multiple_of(g * HD, HD), HD)
            vt[...] = ov[:, cols].T

            def pair(h, carry):
                fold(PAIR_TILES, g, q, ok.at[:, cols], vt, acc_out, stat_out, 2 * h)
                return carry

            lax.fori_loop(0, GROUP // 2, pair, 0)

            @pl.when(later[g] == 0)
            def _():
                write_out(g, acc_out, stat_out, outs)
                finish(g).start()

        return carry

    lax.fori_loop(0, KVH, head, 0)
    for g in range(KVH):
        pl.when(jnp.logical_and(meta[local_at + g] > 0, later[g] == 0))(finish(g).wait)
    for own in (False, True):
        cut_copies("wait", own, *args)


def wide(g):
    return pl.ds(pl.multiple_of(g * WIDE, WIDE), WIDE)


def part(g, j):
    return pl.ds(pl.multiple_of(g * WIDE + j * HD, HD), HD)


def count_heads(meta, counts, *spans):
    for g in range(KVH):
        counts[g] = 0

    def count(i, carry):
        g = meta[i]

        @pl.when(g >= 0)
        def _():
            counts[g] = counts[g] + 1

        return carry

    for span in spans:
        lax.fori_loop(*span, count, 0)


def write_out(g, acc, stat, outs):
    def head(j, carry):
        total = stat[g, GROUP + j]
        outs[g, :, pl.ds(pl.multiple_of(j * HD, HD), HD)] = (acc[g, j] / total).astype(jnp.bfloat16).T
        return carry

    lax.fori_loop(0, GROUP, head, 0)


def fold(tiles, g, q, k, vt, acc, stat, base=0):
    low = lax.broadcasted_iota(jnp.int32, (TILE, TILE), 1) >= lax.broadcasted_iota(jnp.int32, (TILE, TILE), 0)
    peaks, sums, scores, weights = {}, {}, {}, {}
    fresh = {t[:2] for t in tiles if t[5]}
    for j, r in {t[:2]: None for t in tiles if t[:2] not in fresh}:
        at = slice(r * TILE, (r + 1) * TILE)
        peaks[j, r], sums[j, r] = stat[g, base + j, :, at], stat[g, base + GROUP + j, :, at]

    def score(j, r, lo, hi, diagonal, first):
        s = scores_of(k[lo:hi, :], q[r * TILE : (r + 1) * TILE, part(g, base + j)])
        if diagonal:
            last = jnp.where(low, s[hi - lo - TILE :], -1e30)
            s = jnp.concatenate([s[: hi - lo - TILE], last], axis=0) if hi - lo > TILE else last
        return s

    def weigh(s, j, r, lo, hi, diagonal, first):
        m = jnp.max(s, axis=0, keepdims=True)
        m = m if first else jnp.maximum(peaks[j, r], m)
        w = jnp.exp2((s - m) * SCALE)
        total = jnp.sum(w, axis=0, keepdims=True)
        alpha = None
        if not first:
            alpha = jnp.exp2((peaks[j, r] - m) * SCALE)
            total = total + sums[j, r] * alpha
        peaks[j, r], sums[j, r] = m, total
        return w, alpha

    def gather(pair, j, r, lo, hi, diagonal, first):
        w, alpha = pair
        at = slice(r * TILE, (r + 1) * TILE)
        new = total_of(vt[:, lo:hi], w)
        acc[g, base + j, :, at] = new if first else acc[g, base + j, :, at] * alpha + new

    count = len(tiles)
    for t in range(count + 3):
        if t < count:
            scores[t] = score(*tiles[t])
        if 0 <= t - 2 < count:
            weights[t - 2] = weigh(scores.pop(t - 2), *tiles[t - 2])
        if 0 <= t - 3:
            gather(weights.pop(t - 3), *tiles[t - 3])
    for (j, r), m in peaks.items():
        at = slice(r * TILE, (r + 1) * TILE)
        stat[g, base + j, :, at] = m
        stat[g, base + GROUP + j, :, at] = sums[j, r]


def far_kernel(n_here, n_swap, here_at, here_later, swap_at, swap_later, meta, *refs):
    arrived, refs = refs[:n_here], refs[n_here:]
    swapped, refs = refs[:n_swap], refs[n_swap:]
    q, acc, stat, _, acc_out, stat_out, out, outs, kv, vt, seen, here, later, kv_sem, out_sem = refs
    pieces = n_here + (swapped[0].shape[0] // (2 * BLK) if n_swap else 0)

    def finish(g):
        return pltpu.make_async_copy(outs.at[g], out.at[:, wide(g)], out_sem.at[g])

    for i in range(pieces):
        g = meta[here_at + i] if i < n_here else meta[swap_at + i - n_here]
        block = arrived[i] if i < n_here else swapped[0].at[pl.ds((i - n_here) * 2 * BLK, 2 * BLK), :]
        pl.when(g >= 0)(pltpu.make_async_copy(block, kv.at[i], kv_sem.at[i]).start)

    count_heads(meta, here, (here_at, here_at + n_here), (swap_at, swap_at + pieces - n_here))
    count_heads(meta, later, here_later, swap_later)
    for g in range(KVH):
        seen[g] = 0

        @pl.when(jnp.logical_and(later[g] > 0, here[g] == 0))
        def _():
            acc_out[g] = acc[g]
            stat_out[g] = stat[g]

    def piece(i, carry):
        g = meta[jnp.where(i < n_here, here_at + i, swap_at + i - n_here)]

        @pl.when(g >= 0)
        def _():
            @pl.when(seen[g] == 0)
            def _():
                acc_out[g] = acc[g]
                stat_out[g] = stat[g]

            pltpu.make_async_copy(kv.at[i], kv.at[i], kv_sem.at[i]).wait()
            vt[...] = kv[i, BLK:, :].T

            def pair(h, carry):
                fold(PAIR_TILES, g, q, kv.at[i, pl.ds(0, BLK), :], vt, acc_out, stat_out, 2 * h)
                return carry

            lax.fori_loop(0, GROUP // 2, pair, 0)
            seen[g] = seen[g] + 1

            @pl.when(jnp.logical_and(seen[g] == here[g], later[g] == 0))
            def _():
                write_out(g, acc_out, stat_out, outs)
                finish(g).start()

        return carry

    lax.fori_loop(0, pieces, piece, 0)
    for g in range(KVH):
        pl.when(jnp.logical_and(here[g] > 0, later[g] == 0))(finish(g).wait)


def pack_kernel(count, *refs):
    joined = refs[count + 1]
    for i in range(count):
        joined[i * 2 * BLK : (i + 1) * 2 * BLK, :] = refs[i][...]
    refs[count + 2][...] = refs[count][...]


def body(queries, key, value, selection):
    me, side = lax.axis_index("ctx"), lax.axis_index("head")
    peers = lax.axis_size("ctx")
    order, table, groups = patterns(peers)
    total = len(order)
    swap = [(0, 1), (1, 0)]
    okey, ovalue = lax.ppermute(key, "head", swap), lax.ppermute(value, "head", swap)

    ends = lax.dynamic_index_in_dim(jnp.asarray(table), me, 0, keepdims=False)
    targets, sources = ends[:total], ends[total:]
    picks = selection[:, :, 1:]
    asked = lax.dynamic_slice_in_dim(picks, side * KVG, KVG, 1)
    codes = (asked - 2 * me) * KVH + (side * KVG + jnp.arange(KVG, dtype=jnp.int32))[None, :, None] + 1
    wanted = jnp.max(
        jnp.where((asked >> 1) == me, codes, 0).reshape(peers, 2 * KVG * TOPK), axis=1
    )
    cuts = jnp.max(
        jnp.where(targets[:, None] == jnp.arange(peers, dtype=jnp.int32)[None, :], wanted[None, :], 0), axis=1
    )
    mine = lax.dynamic_slice_in_dim(picks, 2 * me + side, 1, 0)[0]
    owners = jnp.where(mine >= 0, mine >> 1, -1)
    local = jnp.any(owners == me, axis=1).astype(jnp.int32)
    heads = jnp.arange(KVH, dtype=jnp.int32)
    hit = jnp.any(owners[None, :, :] == sources[:, None, None], axis=2)
    near = (heads // KVG) == side
    work_here = jnp.max(jnp.where(hit & near, heads, -1), axis=1)
    work_swap = jnp.max(jnp.where(hit & ~near, heads, -1), axis=1)
    meta = jnp.concatenate([side[None].astype(jnp.int32), cuts, local, work_here, work_swap])
    local_at = 1 + total
    here_at = local_at + KVH
    swap_at = here_at + total
    end = swap_at + total

    piece_shape = jax.ShapeDtypeStruct((2 * BLK, HD), jnp.bfloat16)
    any_spec, vmem_spec = pl.BlockSpec(memory_space=ANY), pl.BlockSpec(memory_space=VMEM)
    state = (
        jax.ShapeDtypeStruct((KVH, GROUP, HD, BLK), jnp.float32),
        jax.ShapeDtypeStruct((KVH, 2 * GROUP, 1, BLK), jnp.float32),
        jax.ShapeDtypeStruct((BLK, QH * HD), jnp.bfloat16),
    )
    params = pltpu.CompilerParams(vmem_limit_bytes=16 << 20)

    firsts = [0, groups[1][1], groups[2][1], groups[3][1]]
    counts = [b - a for a, b in zip(firsts[:-1], firsts[1:])]
    def cut(first, count, *through):
        return pl.pallas_call(
            functools.partial(cut_kernel, first, count),
            grid_spec=pltpu.PrefetchScalarGridSpec(
                num_scalar_prefetch=1,
                grid=(),
                in_specs=[vmem_spec] * (4 + len(through)),
                out_specs=[vmem_spec] * len(through) + [any_spec] * count,
                scratch_shapes=[pltpu.SemaphoreType.DMA((count, 2))],
            ),
            out_shape=[*[state[1]] * len(through), *[piece_shape] * count],
            input_output_aliases={5 + i: i for i in range(len(through))},
            compiler_params=params,
            cost_estimate=pl.CostEstimate(flops=0, bytes_accessed=1 << 10, transcendentals=0),
            name="cut",
        )(meta, key, value, okey, ovalue, *through)

    sent = cut(0, counts[0])

    def inner(kernel, name, first, count, *through):
        return pl.pallas_call(
            functools.partial(kernel, local_at, (here_at, end), first),
            grid_spec=pltpu.PrefetchScalarGridSpec(
                num_scalar_prefetch=1,
                grid=(),
                in_specs=[vmem_spec] * 5 + [vmem_spec, vmem_spec, any_spec][: len(through)],
                out_specs=[vmem_spec, vmem_spec] + [any_spec] * (1 + count),
                scratch_shapes=[
                    VMEM((HD, BLK), jnp.bfloat16),
                    VMEM((KVH, BLK, WIDE), jnp.bfloat16),
                    pltpu.SMEM((KVH,), jnp.int32),
                    pltpu.SemaphoreType.DMA((KVH,)),
                    pltpu.SemaphoreType.DMA((count, 2)),
                ],
            ),
            out_shape=(*state, *[piece_shape] * count),
            input_output_aliases={6 + i: i for i in range(len(through))},
            compiler_params=params,
            cost_estimate=pl.CostEstimate(
                flops=0, bytes_accessed=1 << 10, transcendentals=0
            ),
            name=name,
        )(meta, queries, key, value, okey, ovalue, *through)

    acc, stat, out, *second = inner(own_kernel, "own", firsts[1], counts[1])
    sent = [*sent, *second]

    landed = [None] * total
    swapped = []

    def send(n):
        a, b = groups[n]
        for j in range(a, b):
            landed[j] = lax.ppermute(sent[j], "ctx", order[j])

    def pack(n, stat):
        a, b = groups[n]
        count = b - a
        joined, stat = pl.pallas_call(
            functools.partial(pack_kernel, count),
            in_specs=[vmem_spec] * (count + 1),
            out_specs=[vmem_spec] * 2,
            out_shape=(jax.ShapeDtypeStruct((count * 2 * BLK, HD), jnp.bfloat16), state[1]),
            input_output_aliases={count: 1},
            compiler_params=params,
            cost_estimate=pl.CostEstimate(flops=0, bytes_accessed=1 << 10, transcendentals=0),
            name="pack",
        )(*landed[a:b], stat)
        swapped.append(lax.ppermute(joined, "head", swap))
        return stat

    def far(here, swaps, acc, stat, out):
        a, b = groups[here] if here is not None else (0, 0)
        a0, b0 = groups[swaps] if swaps is not None else (0, 0)
        here_end = max(b, b0)
        swap_end = b0 if swaps is not None else a
        n_here = b - a
        pieces = n_here + b0 - a0
        others = [swapped[swaps]] if swaps is not None else []
        base = 1 + n_here + len(others)
        return pl.pallas_call(
            functools.partial(
                far_kernel, n_here, len(others),
                here_at + a, (here_at + here_end, swap_at), swap_at + a0, (swap_at + swap_end, end),
            ),
            grid_spec=pltpu.PrefetchScalarGridSpec(
                num_scalar_prefetch=1,
                grid=(),
                in_specs=[any_spec] * (base - 1) + [vmem_spec] * 3 + [any_spec],
                out_specs=[vmem_spec, vmem_spec, any_spec],
                scratch_shapes=[
                    VMEM((KVH, BLK, WIDE), jnp.bfloat16),
                    VMEM((pieces, 2 * BLK, HD), jnp.bfloat16),
                    VMEM((HD, BLK), jnp.bfloat16),
                    pltpu.SMEM((KVH,), jnp.int32),
                    pltpu.SMEM((KVH,), jnp.int32),
                    pltpu.SMEM((KVH,), jnp.int32),
                    pltpu.SemaphoreType.DMA((pieces,)),
                    pltpu.SemaphoreType.DMA((KVH,)),
                ],
            ),
            out_shape=state,
            input_output_aliases={base + 1 + i: i for i in range(3)},
            compiler_params=params,
            cost_estimate=pl.CostEstimate(
                flops=32 * pieces * ROWS * BLK * HD, bytes_accessed=pieces << 21, transcendentals=pieces * ROWS * BLK
            ),
            name="far",
        )(meta, *landed[a:b], *others, queries, acc, stat, out)

    for n in range(3):
        send(n)
    stat = pack(0, stat)
    acc, stat, out, *third = inner(near_kernel, "near", firsts[2], counts[2], acc, stat, out)
    sent += third
    send(3)
    last = len(groups) - 1
    acc, stat, out = far(0, None, acc, stat, out)
    acc, stat, out = far(None, 0, acc, stat, out)
    for n in range(1, last + 1):
        stat = pack(n, stat)
        if n == last - 2:
            a, b = groups[last]
            stat, *final = cut(a, b - a, stat)
            sent += final
            send(last)
        acc, stat, out = far(n, None, acc, stat, out)
        acc, stat, out = far(None, n, acc, stat, out)
    return out


def solution(mesh):
    placed = (P(("ctx", "head"), None), P(("ctx", "head"), None), P(("ctx", "head"), None), P())
    return jax.shard_map(
        body, mesh=mesh, in_specs=placed, out_specs=P(("ctx", "head"), None), check_vma=False
    )
```

```python
import functools
import math

import jax
import jax.numpy as jnp
import numpy as np
from jax import lax
from jax.experimental import pallas as pl
from jax.experimental.pallas import tpu as pltpu
from jax.sharding import PartitionSpec as P

QH = 32
KVH = 8
HD = 128
BLK = 512
TOPK = 3
GROUP = QH // KVH
KVG = KVH // 2
WIDE = GROUP * HD
ROWS = GROUP * BLK
SCALE = math.log2(math.e) / math.sqrt(HD)
TILE = 128
SPAN = 256
ALL_TILES = [
    (j, r, lo, lo + SPAN, False, False) for lo in range(0, BLK, SPAN) for j in range(GROUP) for r in range(BLK // TILE)
]
VMEM = pltpu.VMEM
ANY = pl.ANY


def patterns(peers):
    fast = 4 if peers % 4 == 0 else 1
    slow = peers // fast

    def permute(moves, flip):
        pairs = [(a * fast + f, b * fast + (f ^ flip)) for a, b in moves for f in range(fast)]
        return [(a, b) for a, b in pairs if a < b]

    level = [(a, a) for a in range(slow)]
    if (fast, slow) == (4, 4):
        two, one, zero = [(0, 2), (1, 3)], [(0, 3), (1, 2)], [(0, 1), (2, 3)]
        order = [permute(two, 0), permute(one, 0), permute(level, 1)]
        order += [permute(two, 1), permute(one, 1), permute(zero, 0), permute(level, 2)]
        order += [permute(two, 2), permute(one, 2), permute(zero, 1), permute(level, 3)]
        order += [permute(two, 3), permute(zero, 2), permute(zero, 3)]
        order += [permute(one, 3)]
        edges = [0, 3, 7, 11, 14, 15]
    else:
        order = []
        for m in range(fast):
            order += [permute([(a, a + d) for a in range(slow - d)], m) for d in range(1, slow)]
        order += [permute(level, m) for m in range(1, fast)]
        edges = [round(i * len(order) / 5) for i in range(6)]
    table = np.full((peers, 2 * len(order)), -2, np.int32)
    for n, pairs in enumerate(order):
        for a, b in pairs:
            table[a, n] = b
            table[b, len(order) + n] = a
    return order, table, list(zip(edges[:-1], edges[1:]))


def scores_of(k, q):
    return lax.dot_general(k, q, (((1,), (1,)), ((), ())), preferred_element_type=jnp.float32)


def total_of(vt, weights):
    return jnp.dot(vt, weights.astype(jnp.bfloat16), preferred_element_type=jnp.float32)


def cut_copies(act, own, first, meta, key, value, okey, ovalue, outs, sems):
    for j, to in enumerate(outs):
        code = meta[1 + first + j] - 1
        block, head = code // KVH, code % KVH
        col = pl.ds(pl.multiple_of(jnp.maximum(head, 0) * HD, HD), HD)
        flag = jnp.logical_and(code >= 0, (block == meta[0]) if own else (block != meta[0]))
        for t, source in enumerate((key, value) if own else (okey, ovalue)):
            copy = pltpu.make_async_copy(source.at[:, col], to.at[pl.ds(t * BLK, BLK), :], sems.at[j, t])
            pl.when(flag)(copy.start if act == "start" else copy.wait)


def cut_kernel(first, count, meta, key, value, okey, ovalue, *rest):
    *through, sems = rest
    outs = through[len(through) - count :]
    args = (first, meta, key, value, okey, ovalue, outs, sems)
    if len(through) > count:
        through[1][...] = through[0][...]
    for act in ("start", "wait"):
        for own in (False, True):
            cut_copies(act, own, *args)


def own_kernel(local_at, work, first, meta, q, k, v, ok, ov, acc_out, stat_out, out, *rest):
    sent, (vt, outs, later, sems, cut_sems) = rest[:-5], rest[-5:]
    args = (first, meta, k, v, ok, ov, sent, cut_sems)
    for own in (False, True):
        cut_copies("start", own, *args)
    count_heads(meta, later, work)
    for g in range(KVH):
        later[g] = later[g] + meta[local_at + g]
    tiles = []
    for lo in range(0, BLK, SPAN):
        for j in range(GROUP):
            for r in range(lo // TILE, BLK // TILE):
                hi = min(lo + SPAN, (r + 1) * TILE)
                tiles.append((j, r, lo, hi, hi == (r + 1) * TILE, lo == 0))

    def finish(g):
        return pltpu.make_async_copy(outs.at[g], out.at[:, wide(g)], sems.at[g])

    def head(g, carry):
        cols = pl.ds(pl.multiple_of(g * HD, HD), HD)
        vt[...] = v[:, cols].T
        fold(tiles, g, q, k.at[:, cols], vt, acc_out, stat_out)

        @pl.when(later[g] == 0)
        def _():
            write_out(g, acc_out, stat_out, outs)
            finish(g).start()

        return carry

    lax.fori_loop(0, KVH, head, 0)
    for g in range(KVH):
        pl.when(later[g] == 0)(finish(g).wait)
    for own in (False, True):
        cut_copies("wait", own, *args)


def near_kernel(local_at, work, first, meta, q, k, v, ok, ov, acc, stat, _, acc_out, stat_out, out, *rest):
    sent, (vt, outs, later, sems, cut_sems) = rest[:-5], rest[-5:]
    args = (first, meta, k, v, ok, ov, sent, cut_sems)
    for own in (False, True):
        cut_copies("start", own, *args)
    count_heads(meta, later, work)

    def finish(g):
        return pltpu.make_async_copy(outs.at[g], out.at[:, wide(g)], sems.at[g])

    def head(g, carry):
        local = meta[local_at + g] > 0

        @pl.when(jnp.logical_or(local, later[g] > 0))
        def _():
            acc_out[g] = acc[g]
            stat_out[g] = stat[g]

        @pl.when(local)
        def _():
            cols = pl.ds(pl.multiple_of(g * HD, HD), HD)
            vt[...] = ov[:, cols].T
            fold(ALL_TILES, g, q, ok.at[:, cols], vt, acc_out, stat_out)

            @pl.when(later[g] == 0)
            def _():
                write_out(g, acc_out, stat_out, outs)
                finish(g).start()

        return carry

    lax.fori_loop(0, KVH, head, 0)
    for g in range(KVH):
        pl.when(jnp.logical_and(meta[local_at + g] > 0, later[g] == 0))(finish(g).wait)
    for own in (False, True):
        cut_copies("wait", own, *args)


def wide(g):
    return pl.ds(pl.multiple_of(g * WIDE, WIDE), WIDE)


def part(g, j):
    return pl.ds(pl.multiple_of(g * WIDE + j * HD, HD), HD)


def count_heads(meta, counts, *spans):
    for g in range(KVH):
        counts[g] = 0

    def count(i, carry):
        g = meta[i]

        @pl.when(g >= 0)
        def _():
            counts[g] = counts[g] + 1

        return carry

    for span in spans:
        lax.fori_loop(*span, count, 0)


def write_out(g, acc, stat, outs):
    for j in range(GROUP):
        total = stat[g, GROUP + j : GROUP + j + 1, :]
        outs[g, :, j * HD : (j + 1) * HD] = (acc[g, j] / total).astype(jnp.bfloat16).T


def fold(tiles, g, q, k, vt, acc, stat):
    low = lax.broadcasted_iota(jnp.int32, (TILE, TILE), 1) >= lax.broadcasted_iota(jnp.int32, (TILE, TILE), 0)
    peaks, sums, scores, weights = {}, {}, {}, {}
    fresh = {t[:2] for t in tiles if t[5]}
    for j, r in {t[:2]: None for t in tiles if t[:2] not in fresh}:
        at = slice(r * TILE, (r + 1) * TILE)
        peaks[j, r], sums[j, r] = stat[g, j : j + 1, at], stat[g, GROUP + j : GROUP + j + 1, at]

    def score(j, r, lo, hi, diagonal, first):
        s = scores_of(k[lo:hi, :], q[r * TILE : (r + 1) * TILE, part(g, j)])
        if diagonal:
            last = jnp.where(low, s[hi - lo - TILE :], -1e30)
            s = jnp.concatenate([s[: hi - lo - TILE], last], axis=0) if hi - lo > TILE else last
        return s

    def weigh(s, j, r, lo, hi, diagonal, first):
        m = jnp.max(s, axis=0, keepdims=True)
        m = m if first else jnp.maximum(peaks[j, r], m)
        w = jnp.exp2((s - m) * SCALE)
        total = jnp.sum(w, axis=0, keepdims=True)
        alpha = None
        if not first:
            alpha = jnp.exp2((peaks[j, r] - m) * SCALE)
            total = total + sums[j, r] * alpha
        peaks[j, r], sums[j, r] = m, total
        return w, alpha

    def gather(pair, j, r, lo, hi, diagonal, first):
        w, alpha = pair
        at = slice(r * TILE, (r + 1) * TILE)
        new = total_of(vt[:, lo:hi], w)
        acc[g, j, :, at] = new if first else acc[g, j, :, at] * alpha + new

    count = len(tiles)
    for t in range(count + 3):
        if t < count:
            scores[t] = score(*tiles[t])
        if 0 <= t - 2 < count:
            weights[t - 2] = weigh(scores.pop(t - 2), *tiles[t - 2])
        if 0 <= t - 3:
            gather(weights.pop(t - 3), *tiles[t - 3])
    for (j, r), m in peaks.items():
        at = slice(r * TILE, (r + 1) * TILE)
        stat[g, j : j + 1, at] = m
        stat[g, GROUP + j : GROUP + j + 1, at] = sums[j, r]


def far_kernel(n_here, n_swap, here_at, here_later, swap_at, swap_later, meta, *refs):
    arrived, refs = refs[:n_here], refs[n_here:]
    swapped, refs = refs[:n_swap], refs[n_swap:]
    q, acc, stat, _, acc_out, stat_out, out, outs, kv, vt, seen, here, later, kv_sem, out_sem = refs
    pieces = n_here + (swapped[0].shape[0] // (2 * BLK) if n_swap else 0)

    def finish(g):
        return pltpu.make_async_copy(outs.at[g], out.at[:, wide(g)], out_sem.at[g])

    for i in range(pieces):
        g = meta[here_at + i] if i < n_here else meta[swap_at + i - n_here]
        block = arrived[i] if i < n_here else swapped[0].at[pl.ds((i - n_here) * 2 * BLK, 2 * BLK), :]
        pl.when(g >= 0)(pltpu.make_async_copy(block, kv.at[i], kv_sem.at[i]).start)

    count_heads(meta, here, (here_at, here_at + n_here), (swap_at, swap_at + pieces - n_here))
    count_heads(meta, later, here_later, swap_later)
    for g in range(KVH):
        seen[g] = 0

        @pl.when(jnp.logical_and(later[g] > 0, here[g] == 0))
        def _():
            acc_out[g] = acc[g]
            stat_out[g] = stat[g]

    def piece(i, carry):
        g = meta[jnp.where(i < n_here, here_at + i, swap_at + i - n_here)]

        @pl.when(g >= 0)
        def _():
            @pl.when(seen[g] == 0)
            def _():
                acc_out[g] = acc[g]
                stat_out[g] = stat[g]

            pltpu.make_async_copy(kv.at[i], kv.at[i], kv_sem.at[i]).wait()
            vt[...] = kv[i, BLK:, :].T
            fold(ALL_TILES, g, q, kv.at[i, pl.ds(0, BLK), :], vt, acc_out, stat_out)
            seen[g] = seen[g] + 1

            @pl.when(jnp.logical_and(seen[g] == here[g], later[g] == 0))
            def _():
                write_out(g, acc_out, stat_out, outs)
                finish(g).start()

        return carry

    lax.fori_loop(0, pieces, piece, 0)
    for g in range(KVH):
        pl.when(jnp.logical_and(here[g] > 0, later[g] == 0))(finish(g).wait)


def pack_kernel(count, *refs):
    joined = refs[count + 1]
    for i in range(count):
        joined[i * 2 * BLK : (i + 1) * 2 * BLK, :] = refs[i][...]
    refs[count + 2][...] = refs[count][...]


def body(queries, key, value, selection):
    me, side = lax.axis_index("ctx"), lax.axis_index("head")
    peers = lax.axis_size("ctx")
    order, table, groups = patterns(peers)
    total = len(order)
    swap = [(0, 1), (1, 0)]
    okey, ovalue = lax.ppermute(key, "head", swap), lax.ppermute(value, "head", swap)

    ends = lax.dynamic_index_in_dim(jnp.asarray(table), me, 0, keepdims=False)
    targets, sources = ends[:total], ends[total:]
    picks = selection[:, :, 1:]
    asked = lax.dynamic_slice_in_dim(picks, side * KVG, KVG, 1)
    codes = (asked - 2 * me) * KVH + (side * KVG + jnp.arange(KVG, dtype=jnp.int32))[None, :, None] + 1
    wanted = jnp.max(
        jnp.where((asked >> 1) == me, codes, 0).reshape(peers, 2 * KVG * TOPK), axis=1
    )
    cuts = jnp.max(
        jnp.where(targets[:, None] == jnp.arange(peers, dtype=jnp.int32)[None, :], wanted[None, :], 0), axis=1
    )
    mine = lax.dynamic_slice_in_dim(picks, 2 * me + side, 1, 0)[0]
    owners = jnp.where(mine >= 0, mine >> 1, -1)
    local = jnp.any(owners == me, axis=1).astype(jnp.int32)
    heads = jnp.arange(KVH, dtype=jnp.int32)
    hit = jnp.any(owners[None, :, :] == sources[:, None, None], axis=2)
    near = (heads // KVG) == side
    work_here = jnp.max(jnp.where(hit & near, heads, -1), axis=1)
    work_swap = jnp.max(jnp.where(hit & ~near, heads, -1), axis=1)
    meta = jnp.concatenate([side[None].astype(jnp.int32), cuts, local, work_here, work_swap])
    local_at = 1 + total
    here_at = local_at + KVH
    swap_at = here_at + total
    end = swap_at + total

    piece_shape = jax.ShapeDtypeStruct((2 * BLK, HD), jnp.bfloat16)
    any_spec, vmem_spec = pl.BlockSpec(memory_space=ANY), pl.BlockSpec(memory_space=VMEM)
    state = (
        jax.ShapeDtypeStruct((KVH, GROUP, HD, BLK), jnp.float32),
        jax.ShapeDtypeStruct((KVH, 2 * GROUP, BLK), jnp.float32),
        jax.ShapeDtypeStruct((BLK, QH * HD), jnp.bfloat16),
    )
    params = pltpu.CompilerParams(vmem_limit_bytes=16 << 20)

    firsts = [0, groups[0][1], groups[1][1], groups[3][1]]
    counts = [b - a for a, b in zip(firsts[:-1], firsts[1:])]
    def cut(first, count, *through):
        return pl.pallas_call(
            functools.partial(cut_kernel, first, count),
            grid_spec=pltpu.PrefetchScalarGridSpec(
                num_scalar_prefetch=1,
                grid=(),
                in_specs=[vmem_spec] * (4 + len(through)),
                out_specs=[vmem_spec] * len(through) + [any_spec] * count,
                scratch_shapes=[pltpu.SemaphoreType.DMA((count, 2))],
            ),
            out_shape=[*[state[1]] * len(through), *[piece_shape] * count],
            input_output_aliases={5 + i: i for i in range(len(through))},
            compiler_params=params,
            cost_estimate=pl.CostEstimate(flops=0, bytes_accessed=1 << 10, transcendentals=0),
            name="cut",
        )(meta, key, value, okey, ovalue, *through)

    sent = cut(0, counts[0])

    def inner(kernel, name, first, count, *through):
        return pl.pallas_call(
            functools.partial(kernel, local_at, (here_at, end), first),
            grid_spec=pltpu.PrefetchScalarGridSpec(
                num_scalar_prefetch=1,
                grid=(),
                in_specs=[vmem_spec] * 5 + [vmem_spec, vmem_spec, any_spec][: len(through)],
                out_specs=[vmem_spec, vmem_spec] + [any_spec] * (1 + count),
                scratch_shapes=[
                    VMEM((HD, BLK), jnp.bfloat16),
                    VMEM((KVH, BLK, WIDE), jnp.bfloat16),
                    pltpu.SMEM((KVH,), jnp.int32),
                    pltpu.SemaphoreType.DMA((KVH,)),
                    pltpu.SemaphoreType.DMA((count, 2)),
                ],
            ),
            out_shape=(*state, *[piece_shape] * count),
            input_output_aliases={6 + i: i for i in range(len(through))},
            compiler_params=params,
            cost_estimate=pl.CostEstimate(
                flops=0, bytes_accessed=1 << 10, transcendentals=0
            ),
            name=name,
        )(meta, queries, key, value, okey, ovalue, *through)

    acc, stat, out, *second = inner(own_kernel, "own", firsts[1], counts[1])
    sent = [*sent, *second]

    landed = [None] * total
    swapped = []

    def send(n):
        a, b = groups[n]
        for j in range(a, b):
            landed[j] = lax.ppermute(sent[j], "ctx", order[j])

    def pack(n, stat):
        a, b = groups[n]
        count = b - a
        joined, stat = pl.pallas_call(
            functools.partial(pack_kernel, count),
            in_specs=[vmem_spec] * (count + 1),
            out_specs=[vmem_spec] * 2,
            out_shape=(jax.ShapeDtypeStruct((count * 2 * BLK, HD), jnp.bfloat16), state[1]),
            input_output_aliases={count: 1},
            compiler_params=params,
            cost_estimate=pl.CostEstimate(flops=0, bytes_accessed=1 << 10, transcendentals=0),
            name="pack",
        )(*landed[a:b], stat)
        swapped.append(lax.ppermute(joined, "head", swap))
        return stat

    def far(here, swaps, acc, stat, out):
        a, b = groups[here] if here is not None else (0, 0)
        a0, b0 = groups[swaps] if swaps is not None else (0, 0)
        here_end = max(b, b0)
        swap_end = b0 if swaps is not None else (groups[here - 1][1] if here else 0)
        n_here = b - a
        pieces = n_here + b0 - a0
        others = [swapped[swaps]] if swaps is not None else []
        base = 1 + n_here + len(others)
        return pl.pallas_call(
            functools.partial(
                far_kernel, n_here, len(others),
                here_at + a, (here_at + here_end, swap_at), swap_at + a0, (swap_at + swap_end, end),
            ),
            grid_spec=pltpu.PrefetchScalarGridSpec(
                num_scalar_prefetch=1,
                grid=(),
                in_specs=[any_spec] * (base - 1) + [vmem_spec] * 3 + [any_spec],
                out_specs=[vmem_spec, vmem_spec, any_spec],
                scratch_shapes=[
                    VMEM((KVH, BLK, WIDE), jnp.bfloat16),
                    VMEM((pieces, 2 * BLK, HD), jnp.bfloat16),
                    VMEM((HD, BLK), jnp.bfloat16),
                    pltpu.SMEM((KVH,), jnp.int32),
                    pltpu.SMEM((KVH,), jnp.int32),
                    pltpu.SMEM((KVH,), jnp.int32),
                    pltpu.SemaphoreType.DMA((pieces,)),
                    pltpu.SemaphoreType.DMA((KVH,)),
                ],
            ),
            out_shape=state,
            input_output_aliases={base + 1 + i: i for i in range(3)},
            compiler_params=params,
            cost_estimate=pl.CostEstimate(
                flops=32 * pieces * ROWS * BLK * HD, bytes_accessed=pieces << 21, transcendentals=pieces * ROWS * BLK
            ),
            name="far",
        )(meta, *landed[a:b], *others, queries, acc, stat, out)

    send(0)
    send(1)
    acc, stat, out, *third = inner(near_kernel, "near", firsts[2], counts[2], acc, stat, out)
    sent += third
    send(2)
    send(3)
    stat = pack(0, stat)
    last = len(groups) - 1
    acc, stat, out = far(0, None, acc, stat, out)
    for n in range(1, last):
        stat = pack(n, stat)
        if n == last - 2:
            a, b = groups[last]
            stat, *final = cut(a, b - a, stat)
            sent += final
            send(last)
        acc, stat, out = far(n, n - 1, acc, stat, out)
    acc, stat, out = far(None, last - 1, acc, stat, out)
    stat = pack(last, stat)
    acc, stat, out = far(last, None, acc, stat, out)
    acc, stat, out = far(None, last, acc, stat, out)
    return out


def solution(mesh):
    placed = (P(("ctx", "head"), None), P(("ctx", "head"), None), P(("ctx", "head"), None), P())
    return jax.shard_map(
        body, mesh=mesh, in_specs=placed, out_specs=P(("ctx", "head"), None), check_vma=False
    )
```
